256 devices in a mesh: ens: 8 (over z), space: 32 (over x, y, core).
Axes of the slice: x: 4, y: 4, z: 8, core: 2. Of those that a mesh axis runs over, the one named last changes fastest.
Arguments:
- initial_states: bfloat16 [8, 100, 98304], P('ens', None, 'space'), may hold values from -6 to 6
- owner: int32 [98304, 1], P('space'), may hold values from 0 to 31; in each aligned block of 3072 rows (0 to 3071, 3072 to 6143, ...) at most 192 rows name the same one
- node_local: int32 [98304], P('space'), may hold values from 0 to 127
- adjacent_vertex_ids: int32 [4096, 16], P('space'), may hold values from 0 to 4095, as said below
- vertex_latents: bfloat16 [4096, 1024], P('space'), may hold values from -6 to 6
- norm_factor: float32 [1024], replicated, may hold values from 0.1 to 1.9
- grid_to_mesh_matrix: bfloat16 [100, 1024], replicated, may hold values from -0.625 to 0.625
- receiver_matrix: bfloat16 [1024, 1024], replicated, may hold values from -0.1875 to 0.1875
- sender_matrix: bfloat16 [1024, 1024], replicated, may hold values from -0.1875 to 0.1875
- link_update_matrix: bfloat16 [1024, 1024], replicated, may hold values from -0.1875 to 0.1875
- mesh_to_grid_matrix: bfloat16 [1024, 100], replicated, may hold values from -0.1875 to 0.1875
- observed: float32 [100, 98304], P(None, 'space'), may hold values from -6 to 6
- area: float32 [98304], P('space'), may hold values from 0.5 to 2
Outputs:
- crps: float32 [100, 98304], P(None, ('space', 'ens'))
- grads: float32 [8, 100, 98304], P('ens', None, 'space')
The draws below stay inside these ranges and needn't reach their ends.
Inputs may be any that keep to these rules, and one draw needn't show every extreme that they name: Among the grid points of one index of space, at most 192 name one owner, and in every draw some owner is named exactly 192 times by one index's points. `adjacent_vertex_ids`: each neighbour of a node lies on the node's own index of space or on the one just before or after it, cyclically: its id divided by 128 is within one of the node's id divided by 128, modulo 32.
All inputs are finite; a program needn't handle non-finite values.
Results may differ from the reference program's by a relative error of at most 0.02.
Values may be sent and summed in bfloat16 or wider, within the bound.
No kernel may reach another device: no remote copies, remote signals or barrier semaphores. Data moves between devices by JAX's collectives and lax.ppermute only.
A program may use at most 128 MiB of HBM per device.

```python
import math
import jax
import jax.numpy as jnp
import numpy as np
from jax import lax

D = 1024
V = 100
K = 16
GRID_DEV = 3072
MESH_DEV = 128
TRAJECTORY_TOTAL = 8
GRID = 98304
MESH = 4096
CAP = 192
N_SPACE = 32


def draw_adjacent_vertex_ids(key, part):
    key = jax.random.fold_in(key, 7)
    first, second = jax.random.split(key)
    rows = jnp.arange(MESH, dtype=jnp.int32)[:, None]
    home = rows // MESH_DEV
    offset = jax.random.randint(first, (MESH, K), -1, 2)
    within = jax.random.randint(second, (MESH, K), 0, MESH_DEV)
    return ((home + offset + N_SPACE) % N_SPACE * MESH_DEV + within).astype(jnp.int32)


def touch_ends(values, key, least, high):
    longest = values.shape.index(max(values.shape))
    spots = []
    for shift in (0, 1):
        where = [jax.random.randint(jax.random.fold_in(key, axis), (), 0, length) for axis, length in enumerate(values.shape)]
        where[longest] = (where[longest] + shift) % values.shape[longest]
        spots.append(tuple(where))
    return values.at[spots[0]].set(least).at[spots[1]].set(high)


def steps_of(rng, extent, cuts, least, top_value):
    def one(position, shards_of):
        heights = jax.random.uniform(jax.random.fold_in(jax.random.fold_in(rng, 6), position), (shards_of,), jnp.float32, least / len(cuts), top_value / len(cuts))
        return jnp.repeat(jnp.exp(heights), extent[position] // shards_of).reshape((-1,) + (1,) * (len(extent) - position - 1))

    level = one(*cuts[0])
    for cut in cuts[1:]:
        level = level * one(*cut)
    return level


def assign_block(rng, own, number, rows, count, top, most, lean):
    order = jax.random.permutation(rng, count)
    heavy_load, common = shares(count, rows * top, most, lean, True), shares(count, rows * top, most, lean, False)
    places = jnp.arange(count)

    def named(lengths, offset_by):
        used = int((lengths > 0).sum())
        fixed = max(1, used // 4)
        shifted = fixed + (places - fixed + offset_by * (used - fixed)) % max(1, count - fixed)
        return jnp.zeros((count,), jnp.int32).at[order[jnp.where(places < fixed, places, shifted)]].set(jnp.asarray(lengths, jnp.int32))

    lengths = jnp.where(number % 4 == 0, named(heavy_load, number // 4), named(common, number - number // 4 - 1))
    mixed = jax.random.permutation(jax.random.fold_in(own, 3), count)
    giver, taker = mixed[0:count // 2 * 2:2], mixed[1:count // 2 * 2:2]
    slack = jnp.minimum(lengths[giver] - 1, most - lengths[taker]) // 2
    slack = jnp.where((giver == order[0]) | (taker == order[0]) | (lengths[taker] == 0), 0, jnp.maximum(slack, 0))
    shifted = jax.random.randint(jax.random.fold_in(own, 4), (count // 2,), 0, 1 << 20) % (slack + 1)
    lengths = lengths.at[giver].add(-shifted).at[taker].add(shifted)
    members = jnp.searchsorted(jnp.cumsum(lengths), jnp.arange(rows * top), side="right").astype(jnp.int32)
    listing = members.reshape(top, rows).T
    listing = listing[jax.random.permutation(jax.random.fold_in(own, 1), rows)]
    offset_by = jax.random.randint(jax.random.fold_in(own, 2), (rows, 1), 0, top)
    return jnp.take_along_axis(listing, (jnp.arange(top)[None, :] + offset_by) % top, axis=1)


def shares(amount, total, limit, skew, full):
    loads = [(1 << 20) // math.isqrt(grade ** skew) + 1 for grade in range(1, amount + 1)]
    largest = limit if full else min(limit, max(-(-total // amount), total * loads[0] // sum(loads)))
    least = 1 if total - largest >= amount - 1 else 0
    holding, spare = [largest] + [least] * (amount - 1), total - largest - least * (amount - 1)
    while spare > 0:
        candidates = [i for i in range(1, amount) if holding[i] < largest] or [i for i in range(1, amount) if holding[i] < limit]
        mass, budget = sum([loads[i] for i in candidates]), spare
        for i in candidates:
            more = min(limit - holding[i], max(1, budget * loads[i] // mass), spare)
            holding[i] = holding[i] + more
            spare = spare - more
    return np.array(holding)


def bell_draw(own_key, extent, width, limit, cuts=(), held_as=jnp.bfloat16):
    result = width * jax.random.normal(own_key, extent, jnp.float32)
    if cuts:
        result = result * steps_of(own_key, extent, cuts, -0.22, 0.18)
    return jnp.clip(result, -limit, limit).astype(held_as)


def setup_inputs(seed: int = 0) -> dict:
    arg_keys = jax.random.split(jax.random.key(seed), 14)
    initial_states = bell_draw(arg_keys[0], (TRAJECTORY_TOTAL, V, GRID), 1.0, 6.0, ((0, 8), (2, 32)))
    owner_keys = jax.random.split(jax.random.fold_in(arg_keys[1], 1), GRID // GRID_DEV)
    owner_turns = jax.random.permutation(jax.random.fold_in(arg_keys[1], 3), GRID // GRID_DEV)
    owner = jax.vmap(lambda own, number: assign_block(jax.random.fold_in(arg_keys[1], 2), own, number, GRID_DEV, N_SPACE, 1, CAP, 2))(owner_keys, owner_turns).reshape((GRID, 1))
    node_local = touch_ends(jax.random.randint(arg_keys[2], (GRID,), 0, MESH_DEV), jax.random.fold_in(arg_keys[2], 1), 0, MESH_DEV - 1).astype(jnp.int32)
    adjacent_vertex_ids = draw_adjacent_vertex_ids(jax.random.fold_in(arg_keys[13], 71), 0)
    vertex_latents = bell_draw(arg_keys[4], (MESH, D), 1.0, 6.0, ((0, 32),))
    norm_factor = jnp.clip(1.0 + 0.18 * jax.random.normal(arg_keys[5], (D,), jnp.float32), 0.1, 1.9)
    grid_to_mesh_matrix = bell_draw(arg_keys[6], (V, D), V ** -0.5, 0.625)
    receiver_matrix = bell_draw(arg_keys[7], (D, D), D ** -0.5, 0.1875)
    sender_matrix = bell_draw(arg_keys[8], (D, D), D ** -0.5, 0.1875)
    link_update_matrix = bell_draw(arg_keys[9], (D, D), D ** -0.5, 0.1875)
    mesh_to_grid_matrix = bell_draw(arg_keys[10], (D, V), D ** -0.5, 0.1875)
    observed = bell_draw(arg_keys[11], (V, GRID), 1.0, 6.0, ((1, 32),), jnp.float32)
    area = jnp.clip(jnp.exp(math.log(2.0) - 1.3862944 * jax.random.uniform(arg_keys[12], (GRID,), jnp.float32) ** steps_of(arg_keys[12], (GRID,), ((0, 32),), -0.2, 0.2)), 0.5, 2.0)
    return dict(initial_states=initial_states, owner=owner, node_local=node_local, adjacent_vertex_ids=adjacent_vertex_ids, vertex_latents=vertex_latents, norm_factor=norm_factor, grid_to_mesh_matrix=grid_to_mesh_matrix, receiver_matrix=receiver_matrix, sender_matrix=sender_matrix, link_update_matrix=link_update_matrix, mesh_to_grid_matrix=mesh_to_grid_matrix, observed=observed, area=area)


def softabs(value):
    return jnp.sqrt(value * value + 0.01)

def predicted_states(trajectory_states, vertex_numbers, adjacent_vertex_ids, vertex_latents, norm_factor, grid_to_mesh_matrix, receiver_matrix, sender_matrix, link_update_matrix, mesh_to_grid_matrix):
    blocks = trajectory_states.reshape(V, N_SPACE, GRID_DEV).transpose(1, 0, 2)
    id_blocks = vertex_numbers.reshape(N_SPACE, GRID_DEV)

    def add_block(total, pair):
        part_fields, part_ids = pair
        embedded = jax.nn.silu(lax.dot_general(part_fields, grid_to_mesh_matrix, (((0,), (0,)), ((), ())), preferred_element_type=jnp.float32))
        return (total + jax.ops.segment_sum(embedded, part_ids, MESH), None)
    node_sum, _ = lax.scan(add_block, jnp.zeros((MESH, D), jnp.float32), (blocks, id_blocks))
    state = vertex_latents.astype(jnp.float32) + node_sum
    centred = state - lax.optimization_barrier(jnp.mean(state, axis=-1, keepdims=True))
    spread = lax.optimization_barrier(jnp.mean(centred * centred, axis=-1, keepdims=True))
    normed = (centred * lax.rsqrt(spread + 1e-05) * norm_factor).astype(jnp.bfloat16)
    query = jnp.dot(normed, receiver_matrix, preferred_element_type=jnp.float32)
    source = jnp.dot(normed, sender_matrix, preferred_element_type=jnp.float32).astype(jnp.bfloat16)

    def node_block(pair):
        query_block, near_block = pair
        picked = source[near_block].astype(jnp.float32)
        edge = jax.nn.silu(query_block[:, None, :] + picked).astype(jnp.bfloat16)
        sent = jax.nn.silu(jnp.dot(edge.reshape(-1, D), link_update_matrix, preferred_element_type=jnp.float32))
        return sent.reshape(MESH_DEV, K, D).sum(1) / K
    message = lax.map(node_block, (query.reshape(N_SPACE, MESH_DEV, D), adjacent_vertex_ids.reshape(N_SPACE, MESH_DEV, K))).reshape(MESH, D)
    updated = (normed.astype(jnp.float32) + message).astype(jnp.bfloat16)
    decoded = lax.dot_general(mesh_to_grid_matrix, updated, (((0,), (1,)), ((), ())), preferred_element_type=jnp.float32).astype(jnp.bfloat16)
    return trajectory_states.astype(jnp.float32) + decoded[:, vertex_numbers].astype(jnp.float32)

def fair_crps(trajectory_list, observed, area):
    count = trajectory_list.shape[0]
    total = jnp.zeros(trajectory_list.shape[1:], jnp.float32)
    slope = jnp.zeros(trajectory_list.shape, jnp.float32)
    for other in range(count):
        diff = trajectory_list - trajectory_list[other][None]
        spread = softabs(diff)
        total = total + lax.optimization_barrier(jnp.sum(spread, axis=0))
        slope = slope + diff / spread
    miss = trajectory_list - observed[None]
    near = softabs(miss)
    crps = area[None, :] * (lax.optimization_barrier(jnp.sum(near, axis=0)) / count - total / (2.0 * count * (count - 1)))
    grads = area[None, None, :] * (miss / near - slope / (count - 1))
    return (crps, grads)

def reference(initial_states, owner, node_local, adjacent_vertex_ids, vertex_latents, norm_factor, grid_to_mesh_matrix, receiver_matrix, sender_matrix, link_update_matrix, mesh_to_grid_matrix, observed, area):
    vertex_numbers = (owner[:, 0] * MESH_DEV + node_local).astype(jnp.int32)
    trajectory_list = jnp.stack([predicted_states(initial_states[trajectory_number], vertex_numbers, adjacent_vertex_ids, vertex_latents, norm_factor, grid_to_mesh_matrix, receiver_matrix, sender_matrix, link_update_matrix, mesh_to_grid_matrix) for trajectory_number in range(TRAJECTORY_TOTAL)])
    crps, grads = fair_crps(trajectory_list, observed, area)
    return (crps, grads)
```

```python
import functools

import jax
import jax.numpy as jnp
from jax import lax
from jax.experimental import pallas as pl
from jax.experimental.pallas import tpu as pltpu
from jax.sharding import PartitionSpec as P

SLOTS = 192
LANE = 128
PART = 13
PAD = 16
BF16, F32 = jnp.bfloat16, jnp.float32
VM = pl.BlockSpec(memory_space=pltpu.VMEM)
SM = pl.BlockSpec(memory_space=pltpu.SMEM)


ANY = pl.BlockSpec(memory_space=pl.ANY)


def cost(flops, moved, transcendentals=0):
    return pl.CostEstimate(flops=int(flops), bytes_accessed=int(moved), transcendentals=int(transcendentals))


def params(mib):
    return pltpu.CompilerParams(vmem_limit_bytes=mib * 2**20)


def pack_kernel(core_ref, own_ref, owner_ref, local_ref, slots_ref, ids_ref, wide, rows, slots, pos_v, pos_s, sem):
    variables = own_ref.shape[0]
    blocks = owner_ref.shape[0]
    spaces = slots.shape[0] // SLOTS
    row = lax.broadcasted_iota(jnp.int32, (LANE, 2 * LANE), 0)
    col = lax.broadcasted_iota(jnp.int32, (LANE, 2 * LANE), 1)
    before = jnp.where((row < col) | (col >= LANE), 1.0, 0.0).astype(BF16)
    names = lax.broadcasted_iota(jnp.int32, (spaces, LANE), 0)
    carry = jnp.zeros((spaces, LANE), F32)
    for j in range(blocks):
        owner = owner_ref[j : j + 1, :]
        hot = jnp.where(names == owner, 1.0, 0.0)
        counts = jnp.dot(hot.astype(BF16), before, preferred_element_type=F32)
        rank = jnp.sum(hot * (counts[:, :LANE] + carry), axis=0, keepdims=True)
        carry = carry + counts[:, LANE:]
        pos_v[j : j + 1, :] = owner * SLOTS + rank.astype(jnp.int32)
    side = jnp.where(owner_ref[...] % 2 == core_ref[0], 0, spaces // 2)
    ids_ref[...] = (side + owner_ref[...] // 2) * LANE + local_ref[...]
    copy = pltpu.make_async_copy(pos_v, pos_s, sem)
    copy.start()
    slots[...] = jnp.zeros_like(slots)
    wide[variables:, :] = jnp.zeros((LANE - variables, wide.shape[1]), F32)
    wide[:variables, :] = own_ref[...].astype(F32)
    for j in range(blocks):
        wide[variables : variables + 1, j * LANE : (j + 1) * LANE] = local_ref[j : j + 1, :].astype(F32)
    for j in range(blocks):
        rows[j * LANE : (j + 1) * LANE, :] = wide[:, j * LANE : (j + 1) * LANE].T
    copy.wait()

    def place(j, _):
        for i in range(0, LANE, 16):
            base = pl.multiple_of(j * LANE + i, 16)
            held = [rows[pl.ds(base + k, 1), :] for k in range(16)]
            for k in range(16):
                slots[pl.ds(pos_s[j, i + k], 1), :] = held[k]
        return 0

    lax.fori_loop(0, blocks, place, 0)
    slots_ref[...] = slots[...].astype(BF16)


def spread_kernel(own_ref, after_ref, parts_ref, wide):
    variables = own_ref.shape[0]
    wide[...] = own_ref[...].astype(F32)
    for c in range(parts_ref.shape[0]):
        held = min(PART, variables - c * PART)
        piece = wide[c * PART : c * PART + held, :]
        parts_ref[c] = jnp.concatenate([piece, jnp.zeros((PAD - held, wide.shape[1]), F32)], axis=0).astype(BF16)


def encode_kernel(
    slots_ref,
    embed_ref,
    latent_ref,
    gain_ref,
    receiver_ref,
    sender_ref,
    normed_ref,
    query_ref,
    source_ref,
    turned,
    total,
    receiver,
    sender,
    sems,
):
    copies = [
        pltpu.make_async_copy(sender_ref, sender, sems.at[0]),
        pltpu.make_async_copy(receiver_ref, receiver, sems.at[1]),
    ]
    for copy in copies:
        copy.start()
    variables = embed_ref.shape[0]
    width = embed_ref.shape[1]
    chunk = 512
    half = jnp.concatenate([embed_ref[...].astype(F32) * 0.5, jnp.zeros((LANE - variables, width), F32)], axis=0)
    turned[...] = half.T.astype(BF16)
    total[...] = jnp.zeros_like(total)
    lanes = lax.broadcasted_iota(jnp.int32, (chunk, LANE), 1).astype(F32)

    def step(c, _):
        x = slots_ref[pl.ds(pl.multiple_of(c * chunk, chunk), chunk), :]
        h = lax.dot_general(turned[...], x, (((1,), (1,)), ((), ())), preferred_element_type=F32)
        act = (h + h * jnp.tanh(h)).astype(BF16)
        node = x[:, variables : variables + 1].astype(F32)
        hot = jnp.where(node == lanes, 1.0, 0.0).astype(BF16)
        total[...] += jnp.dot(act, hot, preferred_element_type=F32)
        return 0

    lax.fori_loop(0, slots_ref.shape[0] // chunk, step, 0)
    state = latent_ref[...].astype(F32) + total[...].T
    centred = state - jnp.mean(state, axis=-1, keepdims=True)
    spread = jnp.mean(centred * centred, axis=-1, keepdims=True)
    normed = (centred * lax.rsqrt(spread + 1e-05) * gain_ref[...]).astype(BF16)
    normed_ref[...] = normed
    copies[0].wait()
    source_ref[...] = jnp.dot(normed, sender[...], preferred_element_type=F32).astype(BF16)
    copies[1].wait()
    query_ref[...] = jnp.dot(normed, receiver[...], preferred_element_type=F32)


def process_kernel(
    near_ref,
    query_ref,
    normed_ref,
    sibling_ref,
    own_ref,
    other_ref,
    link_ref,
    decode_ref,
    behind_ref,
    out_ref,
    beside,
    total,
    spaced,
    link,
    sem,
):
    copy = pltpu.make_async_copy(link_ref, link, sem)
    copy.start()
    nodes, fanout = near_ref.shape
    variables = decode_ref.shape[1]
    group = 4
    beside[:nodes, :] = sibling_ref[...]
    beside[nodes : 2 * nodes, :] = own_ref[...]
    beside[2 * nodes :, :] = other_ref[...]
    lanes = lax.broadcasted_iota(jnp.int32, (nodes, 3 * nodes), 1)
    for g in range(0, fanout, group):
        hot = jnp.concatenate(
            [jnp.where(near_ref[:, k : k + 1] == lanes, 1.0, 0.0) for k in range(g, g + group)], axis=0
        ).astype(BF16)
        picked = jnp.dot(hot, beside[...], preferred_element_type=F32)
        h = 0.5 * (picked + jnp.concatenate([query_ref[...]] * group, axis=0))
        edge = (h + h * jnp.tanh(h)).astype(BF16)
        if g == 0:
            copy.wait()
        z = jnp.dot(edge, link[...], preferred_element_type=F32)
        z = z + z * jnp.tanh(0.5 * z)
        part = sum(z[k * nodes : (k + 1) * nodes] for k in range(group))
        if g == 0:
            total[...] = part
        else:
            total[...] += part
    updated = (normed_ref[...].astype(F32) + total[...] * (0.5 / fanout)).astype(BF16)
    decoded = lax.dot_general(decode_ref[...], updated, (((0,), (1,)), ((), ())), preferred_element_type=F32)
    spaced[...] = jnp.zeros_like(spaced)
    for c in range(out_ref.shape[0]):
        held = min(PART, variables - c * PART)
        spaced[c * PAD : c * PAD + held, :] = decoded[c * PART : c * PART + held, :]
    for c in range(out_ref.shape[0]):
        out_ref[c] = spaced[c * PAD : (c + 1) * PAD, :].astype(BF16)


def crps_kernel(
    member_ref,
    ids_ref,
    table_ref,
    other_ref,
    parts_ref,
    observed_ref,
    area_ref,
    out_ref,
    table,
    states,
    slopes,
    picked,
    held,
    seen,
):
    members = parts_ref.shape[0]
    blocks = ids_ref.shape[0]
    per_member = blocks // members
    variables = observed_ref.shape[0]
    for c in range(members):

        @pl.when(member_ref[0] == c)
        def _():
            count = min(PART, variables - c * PART)
            seen[...] = jnp.zeros_like(seen)
            seen[:count, :] = observed_ref[c * PART : c * PART + count, :]

    rows = out_ref.shape[1]
    half = table_ref.shape[0]
    table[:half, :] = table_ref[...].astype(F32)
    table[half:, :] = other_ref[...].astype(F32)
    for m in range(members):
        states[m * PAD : (m + 1) * PAD, :] = parts_ref[m].astype(F32)
        slopes[m * rows + rows - 8 : (m + 1) * rows, :] = jnp.zeros((8, LANE), F32)

    def block(j, _):
        for i in range(0, LANE, 16):
            row = [table[pl.ds(ids_ref[j, i + k], 1), :] for k in range(16)]
            for k in range(16):
                picked[i + k : i + k + 1, :] = row[k]
        here = pl.ds(pl.multiple_of(j * LANE, LANE), LANE)
        held[...] = picked[...].T + states[:, here]
        area = jnp.broadcast_to(area_ref[pl.ds(j, 1), :], (members, LANE))
        obs = seen[:, here]
        spare = j // per_member * rows + PART * blocks + j % per_member
        for v in range(PART):
            f = held[pl.ds(v, members, stride=PAD), :]
            miss = f - obs[v : v + 1, :]
            q = miss * miss + 0.01
            r = lax.rsqrt(q)
            near = q * r
            slope = None
            pairs = None
            for k in range(1, members // 2 + 1):
                d = f - pltpu.roll(f, k, 0)
                pq = d * d + 0.01
                pr = lax.rsqrt(pq)
                t = d * pr
                s = pq * pr
                if 2 * k < members:
                    t = t - pltpu.roll(t, members - k, 0)
                    s = s + s
                slope = t if slope is None else slope + t
                pairs = s if pairs is None else pairs + s
            slopes[pl.ds(v * blocks + j, members, stride=rows), :] = area * (miss * r - slope * (1.0 / (members - 1)))
            pairs = (pairs + 0.1) * (1.0 / (2.0 * members * (members - 1)))
            value = area * (near * (1.0 / members) - pairs)
            slopes[pl.ds(spare + v * per_member, 1), :] = jnp.sum(value, axis=0, keepdims=True)
        return 0

    lax.fori_loop(0, blocks, block, 0)
    for m in range(members):
        out_ref[m] = slopes[m * rows : (m + 1) * rows, :].astype(BF16)


def unpack_kernel(got_ref, crps_ref, grads_ref, wide):
    variables, points = crps_ref.shape
    parts = got_ref.shape[0]
    per_part = points // LANE
    blocks = parts * per_part
    for c in range(parts):
        wide[...] = got_ref[c].astype(F32)
        held = min(PART, variables - c * PART)
        grads_ref[c * PART * blocks : (c * PART + held) * blocks, :] = wide[: held * blocks, :]
        for j in range(per_part):
            crps_ref[c * PART : c * PART + held, j * LANE : (j + 1) * LANE] = wide[
                pl.ds(PART * blocks + j, held, stride=per_part), :
            ]


def local(
    initial_states,
    owner,
    node_local,
    adjacent_vertex_ids,
    vertex_latents,
    norm_factor,
    grid_to_mesh_matrix,
    receiver_matrix,
    sender_matrix,
    link_update_matrix,
    mesh_to_grid_matrix,
    observed,
    area,
):
    spaces = lax.axis_size("space")
    members = lax.axis_size("ens")
    variables, points = initial_states.shape[1:]
    nodes, width = vertex_latents.shape
    blocks = points // LANE
    shape = jax.ShapeDtypeStruct
    place = lax.axis_index("space")
    core = place % 2
    slots, ids = pl.pallas_call(
        pack_kernel,
        out_shape=(shape((spaces * SLOTS, LANE), BF16), shape((blocks, LANE), jnp.int32)),
        in_specs=[SM] + [VM] * 3,
        out_specs=(VM,) * 2,
        scratch_shapes=[
            pltpu.VMEM((LANE, points), F32),
            pltpu.VMEM((points, LANE), F32),
            pltpu.VMEM((spaces * SLOTS, LANE), F32),
            pltpu.VMEM((blocks, LANE), jnp.int32),
            pltpu.SMEM((blocks, LANE), jnp.int32),
            pltpu.SemaphoreType.DMA,
        ],
        compiler_params=params(24),
        cost_estimate=cost(1.5e8, 8e6),
        name="pack",
    )(core.astype(jnp.int32).reshape(1), initial_states[0], owner.reshape(blocks, LANE), node_local.reshape(blocks, LANE))
    got = lax.all_to_all(slots.reshape(spaces, SLOTS, LANE), "space", split_axis=0, concat_axis=0, tiled=True)
    parts = pl.pallas_call(
        spread_kernel,
        out_shape=shape((members, PAD, points), BF16),
        in_specs=[VM, ANY],
        out_specs=VM,
        scratch_shapes=[pltpu.VMEM((variables, points), F32)],
        compiler_params=params(8),
        cost_estimate=cost(1e6, 2e6),
        name="spread",
    )(initial_states[0], got)
    parts = lax.all_to_all(parts, "ens", split_axis=0, concat_axis=0, tiled=True)
    normed, query, source = pl.pallas_call(
        encode_kernel,
        out_shape=(shape((nodes, width), BF16), shape((nodes, width), F32), shape((nodes, width), BF16)),
        in_specs=[VM] * 4 + [ANY] * 2,
        out_specs=(VM,) * 3,
        scratch_shapes=[
            pltpu.VMEM((width, LANE), BF16),
            pltpu.VMEM((width, nodes), F32),
            pltpu.VMEM((width, width), BF16),
            pltpu.VMEM((width, width), BF16),
            pltpu.SemaphoreType.DMA((2,)),
        ],
        compiler_params=params(32),
        cost_estimate=cost(4e9, 8e6, 6.3e6),
        name="encode",
    )(
        got.reshape(spaces * SLOTS, LANE),
        grid_to_mesh_matrix,
        vertex_latents,
        norm_factor.reshape(1, width),
        receiver_matrix,
        sender_matrix,
    )
    sibling = lax.ppermute(source, "space", [(i, i ^ 1) for i in range(spaces)])
    other = lax.ppermute(source, "space", [(i, (i + 2 * (i % 2) - 1) % spaces) for i in range(spaces)])
    home = adjacent_vertex_ids // nodes
    slab = jnp.where(home == place, 1, jnp.where(home == place + 1 - 2 * core, 0, 2))
    near = slab * nodes + adjacent_vertex_ids % nodes
    decoded = pl.pallas_call(
        process_kernel,
        out_shape=shape((members, PAD, nodes), BF16),
        in_specs=[VM] * 6 + [ANY, VM, ANY],
        out_specs=VM,
        scratch_shapes=[
            pltpu.VMEM((3 * nodes, width), BF16),
            pltpu.VMEM((nodes, width), F32),
            pltpu.VMEM((members * PAD, nodes), F32),
            pltpu.VMEM((width, width), BF16),
            pltpu.SemaphoreType.DMA,
        ],
        compiler_params=params(32),
        cost_estimate=cost(6e9, 4e6, 4.2e6),
        name="process",
    )(near, query, normed, sibling, source, other, link_update_matrix, mesh_to_grid_matrix, parts)
    decoded = lax.all_to_all(decoded, "ens", split_axis=0, concat_axis=0, tiled=True)
    decoded = decoded.reshape(members * PAD, nodes).T
    table = lax.all_to_all(
        jnp.broadcast_to(decoded[None], (spaces // 2, nodes, members * PAD)),
        "space",
        split_axis=0,
        concat_axis=0,
        tiled=True,
        axis_index_groups=[list(range(c, spaces, 2)) for c in range(2)],
    ).reshape(spaces // 2 * nodes, members * PAD)
    table_other = lax.ppermute(table, "space", [(i, i ^ 1) for i in range(spaces)])
    rows = -(-PART * (blocks + blocks // members) // 16) * 16
    slopes = pl.pallas_call(
        crps_kernel,
        out_shape=shape((members, rows, LANE), BF16),
        in_specs=[SM, SM] + [VM] * 5,
        out_specs=VM,
        scratch_shapes=[
            pltpu.VMEM((spaces * nodes, LANE), F32),
            pltpu.VMEM((members * PAD, points), F32),
            pltpu.VMEM((members * rows, LANE), F32),
            pltpu.VMEM((LANE, LANE), F32),
            pltpu.VMEM((members * PAD, LANE), F32),
            pltpu.VMEM((PAD, points), F32),
        ],
        compiler_params=params(24),
        cost_estimate=cost(5e9, 6e6, 2e6),
        name="crps",
    )(
        lax.axis_index("ens").astype(jnp.int32).reshape(1),
        ids,
        table,
        table_other,
        parts,
        observed,
        area.reshape(blocks, LANE),
    )
    slopes = lax.all_to_all(slopes, "ens", split_axis=0, concat_axis=0, tiled=True)
    crps, grads = pl.pallas_call(
        unpack_kernel,
        out_shape=(shape((variables, points // members), F32), shape((variables * blocks, LANE), F32)),
        in_specs=[VM],
        out_specs=(VM, VM),
        scratch_shapes=[pltpu.VMEM((rows, LANE), F32)],
        compiler_params=params(16),
        cost_estimate=cost(1e6, 2e6),
        name="unpack",
    )(slopes)
    return crps, grads.reshape(1, variables, points)


def solution(mesh):
    return jax.shard_map(
        local,
        mesh=mesh,
        in_specs=(
            P("ens", None, "space"),
            P("space", None),
            P("space"),
            P("space", None),
            P("space", None),
            P(),
            P(),
            P(),
            P(),
            P(),
            P(),
            P(None, "space"),
            P("space"),
        ),
        out_specs=(P(None, ("space", "ens")), P("ens", None, "space")),
        check_vma=False,
    )
```

```python
import functools

import jax
import jax.numpy as jnp
from jax import lax
from jax.experimental import pallas as pl
from jax.experimental.pallas import tpu as pltpu
from jax.sharding import PartitionSpec as P

SLOTS = 192
LANE = 128
SENT = 160
PART = 13
PAD = 16
BF16, F32 = jnp.bfloat16, jnp.float32
VM = pl.BlockSpec(memory_space=pltpu.VMEM)
SM = pl.BlockSpec(memory_space=pltpu.SMEM)


HBM = pl.BlockSpec(memory_space=pltpu.HBM)


def cost(flops, moved, transcendentals=0):
    return pl.CostEstimate(flops=int(flops), bytes_accessed=int(moved), transcendentals=int(transcendentals))


def stay(array):
    return pltpu.with_memory_space_constraint(array, pltpu.HBM)


def params(mib):
    return pltpu.CompilerParams(vmem_limit_bytes=mib * 2**20)


def pack_kernel(
    core_ref, own_hbm, owner_hbm, local_hbm, slots_ref, ids_ref, parts_ref, own_ref, owner_ref, local_ref, wide, rows, slots, pos_v, pos_s, sems
):
    loads = [
        pltpu.make_async_copy(owner_hbm, owner_ref, sems.at[0]),
        pltpu.make_async_copy(local_hbm, local_ref, sems.at[1]),
        pltpu.make_async_copy(own_hbm, own_ref, sems.at[2]),
    ]
    for load in loads:
        load.start()
    slots[...] = jnp.zeros_like(slots)
    loads[0].wait()
    loads[1].wait()
    variables = own_ref.shape[0]
    blocks = owner_ref.shape[0]
    spaces = slots.shape[0] // SLOTS
    row = lax.broadcasted_iota(jnp.int32, (LANE, 2 * LANE), 0)
    col = lax.broadcasted_iota(jnp.int32, (LANE, 2 * LANE), 1)
    before = jnp.where((row < col) | (col >= LANE), 1.0, 0.0).astype(BF16)
    names = lax.broadcasted_iota(jnp.int32, (spaces, LANE), 0)
    carry = jnp.zeros((spaces, LANE), F32)
    for j in range(blocks):
        owner = owner_ref[j : j + 1, :]
        hot = jnp.where(names == owner, 1.0, 0.0)
        counts = jnp.dot(hot.astype(BF16), before, preferred_element_type=F32)
        rank = jnp.sum(hot * (counts[:, :LANE] + carry), axis=0, keepdims=True)
        carry = carry + counts[:, LANE:]
        pos_v[j : j + 1, :] = owner * SLOTS + rank.astype(jnp.int32)
    side = jnp.where(owner_ref[...] % 2 == core_ref[0], 0, spaces // 2)
    ids_ref[...] = (side + owner_ref[...] // 2) * LANE + local_ref[...]
    copy = pltpu.make_async_copy(pos_v, pos_s, sems.at[3])
    copy.start()
    loads[2].wait()
    wide[variables:, :] = jnp.zeros((LANE - variables, wide.shape[1]), F32)
    wide[:variables, :] = own_ref[...].astype(F32)
    for c in range(parts_ref.shape[0]):
        held = min(PART, variables - c * PART)
        piece = wide[c * PART : c * PART + held, :]
        parts_ref[c] = jnp.concatenate([piece, jnp.zeros((PAD - held, wide.shape[1]), F32)], axis=0).astype(BF16)
    for j in range(blocks):
        wide[variables : variables + 1, j * LANE : (j + 1) * LANE] = local_ref[j : j + 1, :].astype(F32)
    for j in range(blocks):
        rows[j * LANE : (j + 1) * LANE, :] = wide[:, j * LANE : (j + 1) * LANE].T
    copy.wait()

    def place(j, _):
        for i in range(0, LANE, 16):
            base = pl.multiple_of(j * LANE + i, 16)
            held = [rows[pl.ds(base + k, 1), :] for k in range(16)]
            for k in range(16):
                slots[pl.ds(pos_s[j, i + k], 1), :] = held[k]
        return 0

    lax.fori_loop(0, blocks, place, 0)
    used = variables + 1
    spare = LANE - used
    more = SLOTS - SENT
    lanes = lax.broadcasted_iota(jnp.int32, (more, LANE), 1)
    for o in range(spaces):
        beyond = slots[o * SLOTS + SENT : (o + 1) * SLOTS, :]
        for p in range(SENT // more):
            piece = slots[o * SLOTS + p * more : o * SLOTS + (p + 1) * more, :]
            if p * spare < used:
                piece = jnp.where(lanes >= used, pltpu.roll(beyond, used - p * spare, 1), piece)
            slots_ref[o * SENT + p * more : o * SENT + (p + 1) * more, :] = piece.astype(BF16)


def encode_kernel(
    slots_ref,
    embed_ref,
    latent_ref,
    gain_ref,
    sender_ref,
    normed_ref,
    source_ref,
    beyond,
    sender,
    sem,
):
    copy = pltpu.make_async_copy(sender_ref, sender, sem)
    copy.start()
    variables = embed_ref.shape[0]
    width = embed_ref.shape[1]
    chunk = 512
    half = jnp.concatenate([embed_ref[...].astype(F32) * 0.5, jnp.zeros((LANE - variables, width), F32)], axis=0).astype(BF16)
    lanes = lax.broadcasted_iota(jnp.int32, (chunk, LANE), 1).astype(F32)
    state = latent_ref[...].astype(F32)
    used = variables + 1
    spare = LANE - used
    more = SLOTS - SENT
    place = lax.broadcasted_iota(jnp.int32, (more, LANE), 1)
    for o in range(slots_ref.shape[0] // SENT):
        whole = jnp.zeros((more, LANE), F32)
        for p in range(-(-used // spare)):
            piece = slots_ref[o * SENT + p * more : o * SENT + (p + 1) * more, :].astype(F32)
            there = (place >= p * spare) & (place < (p + 1) * spare)
            whole = jnp.where(there, pltpu.roll(piece, (p * spare - used) % LANE, 1), whole)
        beyond[o * more : (o + 1) * more, :] = whole.astype(BF16)
    whole = slots_ref.shape[0] // chunk
    for c in range(whole + beyond.shape[0] // chunk):
        if c < whole:
            x = slots_ref[c * chunk : (c + 1) * chunk, :]
        else:
            x = beyond[(c - whole) * chunk : (c - whole + 1) * chunk, :]
        h = jnp.dot(x, half, preferred_element_type=F32)
        act = (h + h * jnp.tanh(h)).astype(BF16)
        node = x[:, variables : variables + 1].astype(F32)
        hot = jnp.where(node == lanes, 1.0, 0.0).astype(BF16)
        state = state + lax.dot_general(hot, act, (((0,), (0,)), ((), ())), preferred_element_type=F32)
    centred = state - jnp.mean(state, axis=-1, keepdims=True)
    spread = jnp.mean(centred * centred, axis=-1, keepdims=True)
    normed = (centred * lax.rsqrt(spread + 1e-05) * gain_ref[...]).astype(BF16)
    normed_ref[...] = normed
    copy.wait()
    source_ref[...] = jnp.dot(normed, sender[...], preferred_element_type=F32).astype(BF16)


def near_kernel(
    member_ref,
    near_ref,
    normed_ref,
    sibling_ref,
    own_ref,
    receiver_hbm,
    observed_hbm,
    half_ref,
    seen_ref,
    receiver,
    observed,
    beside,
    sems,
):
    loads = [
        pltpu.make_async_copy(receiver_hbm, receiver, sems.at[0]),
        pltpu.make_async_copy(observed_hbm, observed, sems.at[1]),
    ]
    for load in loads:
        load.start()
    nodes, fanout = near_ref.shape
    group = 4
    beside[:nodes, :] = sibling_ref[...]
    beside[nodes:, :] = own_ref[...]
    lanes = lax.broadcasted_iota(jnp.int32, (nodes, 2 * nodes), 1)
    loads[0].wait()
    query = 0.5 * jnp.dot(normed_ref[...], receiver[...], preferred_element_type=F32)
    for g in range(0, fanout, group):
        hot = jnp.concatenate(
            [jnp.where(near_ref[:, k : k + 1] == lanes, 0.5, 0.0) for k in range(g, g + group)], axis=0
        ).astype(BF16)
        picked = jnp.dot(hot, beside[...], preferred_element_type=F32)
        half_ref[g * nodes : (g + group) * nodes, :] = picked + jnp.concatenate([query] * group, axis=0)
    loads[1].wait()
    variables = observed.shape[0]
    for c in range(-(-variables // PART)):

        @pl.when(member_ref[0] == c)
        def _():
            count = min(PART, variables - c * PART)
            seen_ref[...] = jnp.zeros_like(seen_ref)
            seen_ref[:count, :] = observed[c * PART : c * PART + count, :]


def process_kernel(
    near_ref, half_ref, normed_ref, other_ref, link_ref, decode_ref, out_ref, edges, total, spaced, link, sem
):
    copy = pltpu.make_async_copy(link_ref, link, sem)
    copy.start()
    nodes, fanout = near_ref.shape
    variables = decode_ref.shape[0]
    group = 4
    lanes = lax.broadcasted_iota(jnp.int32, (nodes, nodes), 1) + 2 * nodes
    for g in range(0, fanout, group):
        hot = jnp.concatenate(
            [jnp.where(near_ref[:, k : k + 1] == lanes, 0.5, 0.0) for k in range(g, g + group)], axis=0
        ).astype(BF16)
        h = half_ref[g * nodes : (g + group) * nodes, :] + jnp.dot(hot, other_ref[...], preferred_element_type=F32)
        edges[g * nodes : (g + group) * nodes, :] = (h + h * jnp.tanh(h)).astype(BF16)
    copy.wait()
    for g in range(0, fanout, group):
        z = jnp.dot(edges[g * nodes : (g + group) * nodes, :], link[...], preferred_element_type=F32)
        z = z + z * jnp.tanh(0.5 * z)
        part = sum(z[k * nodes : (k + 1) * nodes] for k in range(group))
        if g == 0:
            total[...] = part
        else:
            total[...] += part
    updated = (normed_ref[...].astype(F32) + total[...] * (0.5 / fanout)).astype(BF16)
    decoded = lax.dot_general(decode_ref[...], updated, (((1,), (1,)), ((), ())), preferred_element_type=F32)
    spaced[...] = jnp.zeros_like(spaced)
    for c in range(out_ref.shape[0]):
        held = min(PART, variables - c * PART)
        spaced[c * PAD : c * PAD + held, :] = decoded[c * PART : c * PART + held, :]
    for c in range(out_ref.shape[0]):
        out_ref[c] = spaced[c * PAD : (c + 1) * PAD, :].astype(BF16)


def crps_kernel(ids_ref, table_ref, other_ref, parts_ref, seen, area_ref, out_ref, table, slopes, picked, held):
    members = parts_ref.shape[0]
    blocks = ids_ref.shape[0]
    per_member = blocks // members
    rows = out_ref.shape[1]
    half = table_ref.shape[0]
    table[:half, :] = table_ref[...].astype(F32)
    table[half:, :] = other_ref[...].astype(F32)
    for m in range(members):
        slopes[m * rows + rows - 8 : (m + 1) * rows, :] = jnp.zeros((8, LANE), F32)
    def fetch(j, turn):
        for i in range(0, LANE, 16):
            row = [table[pl.ds(ids_ref[j, i + k], 1), :] for k in range(16)]
            for k in range(16):
                picked[turn * LANE + i + k : turn * LANE + i + k + 1, :] = row[k]

    def score(j, turn):
        here = pl.ds(pl.multiple_of(j * LANE, LANE), LANE)
        held[turn * LANE : (turn + 1) * LANE, :] = picked[turn * LANE : (turn + 1) * LANE, :].T
        area = area_ref[pl.ds(j, 1), :]
        spare = j // per_member * rows + PART * blocks + j % per_member
        for low in range(0, PAD, 8):
            count = min(8, PART - low)
            start = turn * LANE + low
            f = [
                held[start + m * PAD : start + m * PAD + 8, :] + parts_ref[m, :, here][low : low + 8].astype(F32)
                for m in range(members)
            ]
            obs = seen[low : low + 8, here]
            slope = [None] * members
            pairs = None
            for a in range(members):
                for b in range(a + 1, members):
                    d = f[a] - f[b]
                    q = d * d + 0.01
                    r = lax.rsqrt(q)
                    t = d * r
                    pairs = q * r if pairs is None else pairs + q * r
                    slope[a] = t if slope[a] is None else slope[a] + t
                    slope[b] = -t if slope[b] is None else slope[b] - t
            near = None
            for m in range(members):
                miss = f[m] - obs
                q = miss * miss + 0.01
                r = lax.rsqrt(q)
                near = q * r if near is None else near + q * r
                value = area * (miss * r - slope[m] * (1.0 / (members - 1)))
                slopes[pl.ds(m * rows + low * blocks + j, count, stride=blocks), :] = value[:count]
            pairs = (2.0 * pairs + 0.1 * members) * (1.0 / (2.0 * members * (members - 1)))
            value = area * (near * (1.0 / members) - pairs)
            slopes[pl.ds(spare + low * per_member, count, stride=per_member), :] = value[:count]

    fetch(0, 0)

    def two(i, _):
        fetch(2 * i + 1, 1)
        score(2 * i, 0)
        fetch(jnp.minimum(2 * i + 2, blocks - 1), 0)
        score(2 * i + 1, 1)
        return 0

    lax.fori_loop(0, blocks // 2, two, 0)
    for m in range(members):
        out_ref[m] = slopes[m * rows : (m + 1) * rows, :].astype(BF16)


def unpack_kernel(got_ref, crps_ref, grads_ref, wide):
    variables, points = crps_ref.shape
    parts = got_ref.shape[0]
    per_part = points // LANE
    blocks = parts * per_part
    for c in range(parts):
        wide[...] = got_ref[c].astype(F32)
        held = min(PART, variables - c * PART)
        grads_ref[c * PART * blocks : (c * PART + held) * blocks, :] = wide[: held * blocks, :]
        for j in range(per_part):
            crps_ref[c * PART : c * PART + held, j * LANE : (j + 1) * LANE] = wide[
                pl.ds(PART * blocks + j, held, stride=per_part), :
            ]


def local(
    initial_states,
    owner,
    node_local,
    adjacent_vertex_ids,
    vertex_latents,
    norm_factor,
    grid_to_mesh_matrix,
    receiver_matrix,
    sender_matrix,
    link_update_matrix,
    mesh_to_grid_matrix,
    observed,
    area,
):
    spaces = lax.axis_size("space")
    members = lax.axis_size("ens")
    variables, points = initial_states.shape[1:]
    nodes, width = vertex_latents.shape
    fanout = adjacent_vertex_ids.shape[1]
    blocks = points // LANE
    shape = jax.ShapeDtypeStruct
    place = lax.axis_index("space")
    core = place % 2
    slots, ids, parts = pl.pallas_call(
        pack_kernel,
        out_shape=(
            shape((spaces * SENT, LANE), BF16),
            shape((blocks, LANE), jnp.int32),
            shape((members, PAD, points), BF16),
        ),
        in_specs=[SM] + [HBM] * 3,
        out_specs=(VM,) * 3,
        scratch_shapes=[
            pltpu.VMEM((variables, points), BF16),
            pltpu.VMEM((blocks, LANE), jnp.int32),
            pltpu.VMEM((blocks, LANE), jnp.int32),
            pltpu.VMEM((LANE, points), F32),
            pltpu.VMEM((points, LANE), F32),
            pltpu.VMEM((spaces * SLOTS, LANE), F32),
            pltpu.VMEM((blocks, LANE), jnp.int32),
            pltpu.SMEM((blocks, LANE), jnp.int32),
            pltpu.SemaphoreType.DMA((4,)),
        ],
        compiler_params=params(16),
        cost_estimate=cost(1.5e8, 8e6),
        name="pack",
    )(
        core.astype(jnp.int32).reshape(1),
        stay(initial_states[0]),
        stay(owner.reshape(blocks, LANE)),
        stay(node_local.reshape(blocks, LANE)),
    )
    got = lax.all_to_all(slots.reshape(spaces, SENT, LANE), "space", split_axis=0, concat_axis=0, tiled=True)
    got, parts = lax.optimization_barrier((got, parts))
    parts = lax.all_to_all(parts, "ens", split_axis=0, concat_axis=0, tiled=True)
    normed, source = pl.pallas_call(
        encode_kernel,
        out_shape=(shape((nodes, width), BF16), shape((nodes, width), BF16)),
        in_specs=[VM] * 4 + [HBM],
        out_specs=(VM,) * 2,
        scratch_shapes=[
            pltpu.VMEM((spaces * (SLOTS - SENT), LANE), BF16),
            pltpu.VMEM((width, width), BF16),
            pltpu.SemaphoreType.DMA,
        ],
        compiler_params=params(20),
        cost_estimate=cost(4e9, 8e6, 6.3e6),
        name="encode",
    )(
        got.reshape(spaces * SENT, LANE),
        grid_to_mesh_matrix,
        vertex_latents,
        norm_factor.reshape(1, width),
        stay(sender_matrix),
    )
    sibling = lax.ppermute(source, "space", [(i, i ^ 1) for i in range(spaces)])
    other = lax.ppermute(source, "space", [(i, (i + 2 * (i % 2) - 1) % spaces) for i in range(spaces)])
    home = adjacent_vertex_ids // nodes
    slab = jnp.where(home == place, 1, jnp.where(home == place + 1 - 2 * core, 0, 2))
    near = slab * nodes + adjacent_vertex_ids % nodes
    half, seen = pl.pallas_call(
        near_kernel,
        out_shape=(shape((fanout * nodes, width), F32), shape((PAD, points), F32)),
        in_specs=[SM] + [VM] * 4 + [HBM] * 2,
        out_specs=(VM, VM),
        scratch_shapes=[
            pltpu.VMEM((width, width), BF16),
            pltpu.VMEM((variables, points), F32),
            pltpu.VMEM((2 * nodes, width), BF16),
            pltpu.SemaphoreType.DMA((2,)),
        ],
        compiler_params=params(16),
        cost_estimate=cost(2e9, 4e6),
        name="near",
    )(
        lax.axis_index("ens").astype(jnp.int32).reshape(1),
        near,
        normed,
        sibling,
        source,
        stay(receiver_matrix),
        stay(observed),
    )
    decoded = pl.pallas_call(
        process_kernel,
        out_shape=shape((members, PAD, nodes), BF16),
        in_specs=[VM] * 4 + [HBM, VM],
        out_specs=VM,
        scratch_shapes=[
            pltpu.VMEM((fanout * nodes, width), BF16),
            pltpu.VMEM((nodes, width), F32),
            pltpu.VMEM((members * PAD, nodes), F32),
            pltpu.VMEM((width, width), BF16),
            pltpu.SemaphoreType.DMA,
        ],
        compiler_params=params(20),
        cost_estimate=cost(6e9, 4e6, 4.2e6),
        name="process",
    )(near, half, normed, other, stay(link_update_matrix), mesh_to_grid_matrix.T)
    decoded, parts = lax.optimization_barrier((decoded, parts))
    decoded = lax.all_to_all(decoded, "ens", split_axis=0, concat_axis=0, tiled=True)
    decoded = decoded.reshape(members * PAD, nodes).T
    table = lax.all_to_all(
        jnp.broadcast_to(decoded[None], (spaces // 2, nodes, members * PAD)),
        "space",
        split_axis=0,
        concat_axis=0,
        tiled=True,
        axis_index_groups=[list(range(c, spaces, 2)) for c in range(2)],
    ).reshape(spaces // 2 * nodes, members * PAD)
    table_other = lax.ppermute(table, "space", [(i, i ^ 1) for i in range(spaces)])
    rows = -(-PART * (blocks + blocks // members) // 16) * 16
    slopes = pl.pallas_call(
        crps_kernel,
        out_shape=shape((members, rows, LANE), BF16),
        in_specs=[SM] + [VM] * 5,
        out_specs=VM,
        scratch_shapes=[
            pltpu.VMEM((spaces * nodes, LANE), F32),
            pltpu.VMEM((members * rows, LANE), F32),
            pltpu.VMEM((2 * LANE, LANE), F32),
            pltpu.VMEM((2 * members * PAD, LANE), F32),
        ],
        compiler_params=params(20),
        cost_estimate=cost(5e9, 6e6, 2e6),
        name="crps",
    )(
        ids,
        table,
        table_other,
        parts,
        seen,
        area.reshape(blocks, LANE),
    )
    slopes = lax.all_to_all(slopes, "ens", split_axis=0, concat_axis=0, tiled=True)
    crps, grads = pl.pallas_call(
        unpack_kernel,
        out_shape=(shape((variables, points // members), F32), shape((variables * blocks, LANE), F32)),
        in_specs=[VM],
        out_specs=(VM, VM),
        scratch_shapes=[pltpu.VMEM((rows, LANE), F32)],
        compiler_params=params(16),
        cost_estimate=cost(1e6, 2e6),
        name="unpack",
    )(slopes)
    return crps, grads.reshape(1, variables, points)


def solution(mesh):
    return jax.shard_map(
        local,
        mesh=mesh,
        in_specs=(
            P("ens", None, "space"),
            P("space", None),
            P("space"),
            P("space", None),
            P("space", None),
            P(),
            P(),
            P(),
            P(),
            P(),
            P(),
            P(None, "space"),
            P("space"),
        ),
        out_specs=(P(None, ("space", "ens")), P("ens", None, "space")),
        check_vma=False,
    )
```

```python
import functools

import jax
import jax.numpy as jnp
from jax import lax
from jax.experimental import pallas as pl
from jax.experimental.pallas import tpu as pltpu
from jax.sharding import PartitionSpec as P

SLOTS = 192
LANE = 128
SENT = 160
PART = 13
PAD = 16
BF16, F32 = jnp.bfloat16, jnp.float32
VM = pl.BlockSpec(memory_space=pltpu.VMEM)
SM = pl.BlockSpec(memory_space=pltpu.SMEM)


HBM = pl.BlockSpec(memory_space=pltpu.HBM)


def cost(flops, moved, transcendentals=0):
    return pl.CostEstimate(flops=int(flops), bytes_accessed=int(moved), transcendentals=int(transcendentals))


def stay(array):
    return pltpu.with_memory_space_constraint(array, pltpu.HBM)


def params(mib):
    return pltpu.CompilerParams(vmem_limit_bytes=mib * 2**20)


def pack_kernel(
    core_ref, own_hbm, owner_hbm, local_hbm, slots_ref, ids_ref, *rest
):
    *parts, own_ref, owner_ref, local_ref, wide, rows, slots, flat, pos_v, pos_s, sems = rest
    loads = [
        pltpu.make_async_copy(owner_hbm, owner_ref, sems.at[0]),
        pltpu.make_async_copy(local_hbm, local_ref, sems.at[1]),
        pltpu.make_async_copy(own_hbm, own_ref, sems.at[2]),
    ]
    for load in loads:
        load.start()
    slots[...] = jnp.zeros_like(slots)
    loads[0].wait()
    loads[1].wait()
    variables = own_ref.shape[0]
    blocks = owner_ref.shape[0]
    spaces = slots.shape[0] // SLOTS
    row = lax.broadcasted_iota(jnp.int32, (LANE, 2 * LANE), 0)
    col = lax.broadcasted_iota(jnp.int32, (LANE, 2 * LANE), 1)
    before = jnp.where((row < col) | (col >= LANE), 1.0, 0.0).astype(BF16)
    names = lax.broadcasted_iota(jnp.int32, (spaces, LANE), 0)
    carry = jnp.zeros((spaces, LANE), F32)
    for j in range(blocks):
        owner = owner_ref[j : j + 1, :]
        hot = jnp.where(names == owner, 1.0, 0.0)
        counts = jnp.dot(hot.astype(BF16), before, preferred_element_type=F32)
        rank = jnp.sum(hot * (counts[:, :LANE] + carry), axis=0, keepdims=True)
        carry = carry + counts[:, LANE:]
        pos_v[j : j + 1, :] = owner * SLOTS + rank.astype(jnp.int32)
    side = jnp.where(owner_ref[...] % 2 == core_ref[0], 0, spaces // 2)
    ids_ref[...] = (side + owner_ref[...] // 2) * LANE + local_ref[...]
    copy = pltpu.make_async_copy(pos_v, pos_s, sems.at[3])
    copy.start()
    loads[2].wait()
    wide[variables:, :] = jnp.zeros((LANE - variables, wide.shape[1]), F32)
    wide[:variables, :] = own_ref[...].astype(F32)
    members = len(parts)
    for j in range(blocks):
        for low in range(0, variables, 8):
            count = min(8, variables - low)
            flat[pl.ds(low * blocks + j, count, stride=blocks), :] = wide[low : low + count, j * LANE : (j + 1) * LANE]
    flat[variables * blocks :, :] = jnp.zeros((flat.shape[0] - variables * blocks, LANE), F32)
    for d in range(members):
        first = pl.multiple_of((core_ref[1] + d) % members * (PART * blocks), 8)
        parts[d][...] = flat[pl.ds(first, parts[d].shape[0]), :].astype(BF16)
    for j in range(blocks):
        wide[variables : variables + 1, j * LANE : (j + 1) * LANE] = local_ref[j : j + 1, :].astype(F32)
    for j in range(blocks):
        rows[j * LANE : (j + 1) * LANE, :] = wide[:, j * LANE : (j + 1) * LANE].T
    copy.wait()

    def place(j, _):
        for i in range(0, LANE, 16):
            base = pl.multiple_of(j * LANE + i, 16)
            held = [rows[pl.ds(base + k, 1), :] for k in range(16)]
            for k in range(16):
                slots[pl.ds(pos_s[j, i + k], 1), :] = held[k]
        return 0

    lax.fori_loop(0, blocks, place, 0)
    used = variables + 1
    spare = LANE - used
    more = SLOTS - SENT
    lanes = lax.broadcasted_iota(jnp.int32, (more, LANE), 1)
    for o in range(spaces):
        beyond = slots[o * SLOTS + SENT : (o + 1) * SLOTS, :]
        for p in range(SENT // more):
            piece = slots[o * SLOTS + p * more : o * SLOTS + (p + 1) * more, :]
            if p * spare < used:
                piece = jnp.where(lanes >= used, pltpu.roll(beyond, used - p * spare, 1), piece)
            slots_ref[o * SENT + p * more : o * SENT + (p + 1) * more, :] = piece.astype(BF16)


def encode_kernel(
    slots_ref,
    embed_ref,
    latent_ref,
    gain_ref,
    sender_ref,
    normed_ref,
    source_ref,
    beyond,
    sender,
    sem,
):
    copy = pltpu.make_async_copy(sender_ref, sender, sem)
    copy.start()
    variables = embed_ref.shape[0]
    width = embed_ref.shape[1]
    chunk = 512
    half = jnp.concatenate([embed_ref[...].astype(F32) * 0.5, jnp.zeros((LANE - variables, width), F32)], axis=0).astype(BF16)
    lanes = lax.broadcasted_iota(jnp.int32, (chunk, LANE), 1).astype(F32)
    state = latent_ref[...].astype(F32)
    used = variables + 1
    spare = LANE - used
    more = SLOTS - SENT
    place = lax.broadcasted_iota(jnp.int32, (more, LANE), 1)
    for o in range(slots_ref.shape[0] // SENT):
        whole = jnp.zeros((more, LANE), F32)
        for p in range(-(-used // spare)):
            piece = slots_ref[o * SENT + p * more : o * SENT + (p + 1) * more, :].astype(F32)
            there = (place >= p * spare) & (place < (p + 1) * spare)
            whole = jnp.where(there, pltpu.roll(piece, (p * spare - used) % LANE, 1), whole)
        beyond[o * more : (o + 1) * more, :] = whole.astype(BF16)
    whole = slots_ref.shape[0] // chunk
    for c in range(whole + beyond.shape[0] // chunk):
        if c < whole:
            x = slots_ref[c * chunk : (c + 1) * chunk, :]
        else:
            x = beyond[(c - whole) * chunk : (c - whole + 1) * chunk, :]
        h = jnp.dot(x, half, preferred_element_type=F32)
        act = (h + h * jnp.tanh(h)).astype(BF16)
        node = x[:, variables : variables + 1].astype(F32)
        hot = jnp.where(node == lanes, 1.0, 0.0).astype(BF16)
        state = state + lax.dot_general(hot, act, (((0,), (0,)), ((), ())), preferred_element_type=F32)
    centred = state - jnp.mean(state, axis=-1, keepdims=True)
    spread = jnp.mean(centred * centred, axis=-1, keepdims=True)
    normed = (centred * lax.rsqrt(spread + 1e-05) * gain_ref[...]).astype(BF16)
    normed_ref[...] = normed
    copy.wait()
    source_ref[...] = jnp.dot(normed, sender[...], preferred_element_type=F32).astype(BF16)


def near_kernel(
    member_ref,
    near_ref,
    normed_ref,
    sibling_ref,
    own_ref,
    receiver_hbm,
    observed_hbm,
    half_ref,
    seen_ref,
    receiver,
    observed,
    beside,
    sems,
):
    loads = [
        pltpu.make_async_copy(receiver_hbm, receiver, sems.at[0]),
        pltpu.make_async_copy(observed_hbm, observed, sems.at[1]),
    ]
    for load in loads:
        load.start()
    nodes, fanout = near_ref.shape
    group = 4
    beside[:nodes, :] = sibling_ref[...]
    beside[nodes:, :] = own_ref[...]
    lanes = lax.broadcasted_iota(jnp.int32, (nodes, 2 * nodes), 1)
    loads[0].wait()
    query = 0.5 * jnp.dot(normed_ref[...], receiver[...], preferred_element_type=F32)
    for g in range(0, fanout, group):
        hot = jnp.concatenate(
            [jnp.where(near_ref[:, k : k + 1] == lanes, 0.5, 0.0) for k in range(g, g + group)], axis=0
        ).astype(BF16)
        picked = jnp.dot(hot, beside[...], preferred_element_type=F32)
        half_ref[g * nodes : (g + group) * nodes, :] = picked + jnp.concatenate([query] * group, axis=0)
    loads[1].wait()
    variables = observed.shape[0]
    for c in range(-(-variables // PART)):

        @pl.when(member_ref[0] == c)
        def _():
            count = min(PART, variables - c * PART)
            seen_ref[...] = jnp.zeros_like(seen_ref)
            seen_ref[:count, :] = observed[c * PART : c * PART + count, :]


def process_kernel(
    near_ref, half_ref, normed_ref, other_ref, link_ref, decode_ref, out_ref, edges, total, spaced, link, sem
):
    copy = pltpu.make_async_copy(link_ref, link, sem)
    copy.start()
    nodes, fanout = near_ref.shape
    variables = decode_ref.shape[0]
    group = 4
    lanes = lax.broadcasted_iota(jnp.int32, (nodes, nodes), 1) + 2 * nodes
    for g in range(0, fanout, group):
        hot = jnp.concatenate(
            [jnp.where(near_ref[:, k : k + 1] == lanes, 0.5, 0.0) for k in range(g, g + group)], axis=0
        ).astype(BF16)
        h = half_ref[g * nodes : (g + group) * nodes, :] + jnp.dot(hot, other_ref[...], preferred_element_type=F32)
        edges[g * nodes : (g + group) * nodes, :] = (h + h * jnp.tanh(h)).astype(BF16)
    copy.wait()
    for g in range(0, fanout, group):
        z = jnp.dot(edges[g * nodes : (g + group) * nodes, :], link[...], preferred_element_type=F32)
        z = z + z * jnp.tanh(0.5 * z)
        part = sum(z[k * nodes : (k + 1) * nodes] for k in range(group))
        if g == 0:
            total[...] = part
        else:
            total[...] += part
    updated = (normed_ref[...].astype(F32) + total[...] * (0.5 / fanout)).astype(BF16)
    decoded = lax.dot_general(decode_ref[...], updated, (((1,), (1,)), ((), ())), preferred_element_type=F32)
    spaced[...] = jnp.zeros_like(spaced)
    for c in range(out_ref.shape[0]):
        held = min(PART, variables - c * PART)
        spaced[c * PAD : c * PAD + held, :] = decoded[c * PART : c * PART + held, :]
    for c in range(out_ref.shape[0]):
        out_ref[c] = spaced[c * PAD : (c + 1) * PAD, :].astype(BF16)


def crps_kernel(member_ref, ids_ref, table_ref, other_ref, seen, area_ref, *rest):
    *parts, out_ref, table, states, slopes, picked, held = rest
    members = len(parts)
    names = [(member_ref[0] + members - d) % members for d in range(members)]
    blocks = ids_ref.shape[0]
    per_member = blocks // members
    rows = out_ref.shape[1]
    half = table_ref.shape[0]
    table[:half, :] = table_ref[...].astype(F32)
    table[half:, :] = other_ref[...].astype(F32)
    size = parts[0].shape[0]
    for d in range(members):
        states[d * size : (d + 1) * size, :] = parts[d][...].astype(F32)
    states[members * size :, :] = jnp.zeros((states.shape[0] - members * size, LANE), F32)
    for m in range(members):
        slopes[m * rows + rows - 8 : (m + 1) * rows, :] = jnp.zeros((8, LANE), F32)
    def fetch(j, turn):
        for i in range(0, LANE, 16):
            row = [table[pl.ds(ids_ref[j, i + k], 1), :] for k in range(16)]
            for k in range(16):
                picked[turn * LANE + i + k : turn * LANE + i + k + 1, :] = row[k]

    def score(j, turn):
        here = pl.ds(pl.multiple_of(j * LANE, LANE), LANE)
        held[turn * LANE : (turn + 1) * LANE, :] = picked[turn * LANE : (turn + 1) * LANE, :].T
        area = area_ref[pl.ds(j, 1), :]
        spare = j // per_member * rows + PART * blocks + j % per_member
        for low in range(0, PAD, 8):
            count = min(8, PART - low)
            start = turn * LANE + low
            f = [
                held[pl.ds(pl.multiple_of(start + names[m] * PAD, 8), 8), :] + states[pl.ds(m * size + low * blocks + j, 8, stride=blocks), :]
                for m in range(members)
            ]
            obs = seen[low : low + 8, here]
            slope = [None] * members
            pairs = None
            for a in range(members):
                for b in range(a + 1, members):
                    d = f[a] - f[b]
                    q = d * d + 0.01
                    r = lax.rsqrt(q)
                    t = d * r
                    pairs = q * r if pairs is None else pairs + q * r
                    slope[a] = t if slope[a] is None else slope[a] + t
                    slope[b] = -t if slope[b] is None else slope[b] - t
            near = None
            for m in range(members):
                miss = f[m] - obs
                q = miss * miss + 0.01
                r = lax.rsqrt(q)
                near = q * r if near is None else near + q * r
                value = area * (miss * r - slope[m] * (1.0 / (members - 1)))
                slopes[pl.ds(names[m] * rows + low * blocks + j, count, stride=blocks), :] = value[:count]
            pairs = (2.0 * pairs + 0.1 * members) * (1.0 / (2.0 * members * (members - 1)))
            value = area * (near * (1.0 / members) - pairs)
            slopes[pl.ds(spare + low * per_member, count, stride=per_member), :] = value[:count]

    fetch(0, 0)

    def two(i, _):
        fetch(2 * i + 1, 1)
        score(2 * i, 0)
        fetch(jnp.minimum(2 * i + 2, blocks - 1), 0)
        score(2 * i + 1, 1)
        return 0

    lax.fori_loop(0, blocks // 2, two, 0)
    for m in range(members):
        out_ref[m] = slopes[m * rows : (m + 1) * rows, :].astype(BF16)


def unpack_kernel(got_ref, crps_ref, grads_ref, wide):
    variables, points = crps_ref.shape
    parts = got_ref.shape[0]
    per_part = points // LANE
    blocks = parts * per_part
    for c in range(parts):
        wide[...] = got_ref[c].astype(F32)
        held = min(PART, variables - c * PART)
        grads_ref[c * PART * blocks : (c * PART + held) * blocks, :] = wide[: held * blocks, :]
        for j in range(per_part):
            crps_ref[c * PART : c * PART + held, j * LANE : (j + 1) * LANE] = wide[
                pl.ds(PART * blocks + j, held, stride=per_part), :
            ]


def local(
    initial_states,
    owner,
    node_local,
    adjacent_vertex_ids,
    vertex_latents,
    norm_factor,
    grid_to_mesh_matrix,
    receiver_matrix,
    sender_matrix,
    link_update_matrix,
    mesh_to_grid_matrix,
    observed,
    area,
):
    spaces = lax.axis_size("space")
    members = lax.axis_size("ens")
    variables, points = initial_states.shape[1:]
    nodes, width = vertex_latents.shape
    fanout = adjacent_vertex_ids.shape[1]
    blocks = points // LANE
    shape = jax.ShapeDtypeStruct
    place = lax.axis_index("space")
    core = place % 2
    member = lax.axis_index("ens")
    held = -(-PART * blocks // 16) * 16
    slots, ids, *parts = pl.pallas_call(
        pack_kernel,
        out_shape=(
            shape((spaces * SENT, LANE), BF16),
            shape((blocks, LANE), jnp.int32),
            *[shape((held, LANE), BF16)] * members,
        ),
        in_specs=[SM] + [HBM] * 3,
        out_specs=(VM,) * (2 + members),
        scratch_shapes=[
            pltpu.VMEM((variables, points), BF16),
            pltpu.VMEM((blocks, LANE), jnp.int32),
            pltpu.VMEM((blocks, LANE), jnp.int32),
            pltpu.VMEM((LANE, points), F32),
            pltpu.VMEM((points, LANE), F32),
            pltpu.VMEM((spaces * SLOTS, LANE), F32),
            pltpu.VMEM(((members - 1) * PART * blocks + held, LANE), F32),
            pltpu.VMEM((blocks, LANE), jnp.int32),
            pltpu.SMEM((blocks, LANE), jnp.int32),
            pltpu.SemaphoreType.DMA((4,)),
        ],
        compiler_params=params(16),
        cost_estimate=cost(1.5e8, 8e6),
        name="pack",
    )(
        jnp.stack([core, member]).astype(jnp.int32),
        stay(initial_states[0]),
        stay(owner.reshape(blocks, LANE)),
        stay(node_local.reshape(blocks, LANE)),
    )
    got = lax.all_to_all(slots.reshape(spaces, SENT, LANE), "space", split_axis=0, concat_axis=0, tiled=True)
    for d in (3, 5, 2, 6, 1, 7, 4):
        parts[d] = lax.ppermute(parts[d], "ens", [(i, (i + d) % members) for i in range(members)])
    soon = (3, 5, 2, 6, 1, 7)
    got, *moved = lax.optimization_barrier((got, *[parts[d] for d in soon]))
    for d, part in zip(soon, moved):
        parts[d] = part
    normed, source = pl.pallas_call(
        encode_kernel,
        out_shape=(shape((nodes, width), BF16), shape((nodes, width), BF16)),
        in_specs=[VM] * 4 + [HBM],
        out_specs=(VM,) * 2,
        scratch_shapes=[
            pltpu.VMEM((spaces * (SLOTS - SENT), LANE), BF16),
            pltpu.VMEM((width, width), BF16),
            pltpu.SemaphoreType.DMA,
        ],
        compiler_params=params(20),
        cost_estimate=cost(4e9, 8e6, 6.3e6),
        name="encode",
    )(
        got.reshape(spaces * SENT, LANE),
        grid_to_mesh_matrix,
        vertex_latents,
        norm_factor.reshape(1, width),
        stay(sender_matrix),
    )
    source, parts[4] = lax.optimization_barrier((source, parts[4]))
    sibling = lax.ppermute(source, "space", [(i, i ^ 1) for i in range(spaces)])
    other = lax.ppermute(source, "space", [(i, (i + 2 * (i % 2) - 1) % spaces) for i in range(spaces)])
    home = adjacent_vertex_ids // nodes
    slab = jnp.where(home == place, 1, jnp.where(home == place + 1 - 2 * core, 0, 2))
    near = slab * nodes + adjacent_vertex_ids % nodes
    half, seen = pl.pallas_call(
        near_kernel,
        out_shape=(shape((fanout * nodes, width), F32), shape((PAD, points), F32)),
        in_specs=[SM] + [VM] * 4 + [HBM] * 2,
        out_specs=(VM, VM),
        scratch_shapes=[
            pltpu.VMEM((width, width), BF16),
            pltpu.VMEM((variables, points), F32),
            pltpu.VMEM((2 * nodes, width), BF16),
            pltpu.SemaphoreType.DMA((2,)),
        ],
        compiler_params=params(16),
        cost_estimate=cost(2e9, 4e6),
        name="near",
    )(
        member.astype(jnp.int32).reshape(1),
        near,
        normed,
        sibling,
        source,
        stay(receiver_matrix),
        stay(observed),
    )
    decoded = pl.pallas_call(
        process_kernel,
        out_shape=shape((members, PAD, nodes), BF16),
        in_specs=[VM] * 4 + [HBM, VM],
        out_specs=VM,
        scratch_shapes=[
            pltpu.VMEM((fanout * nodes, width), BF16),
            pltpu.VMEM((nodes, width), F32),
            pltpu.VMEM((members * PAD, nodes), F32),
            pltpu.VMEM((width, width), BF16),
            pltpu.SemaphoreType.DMA,
        ],
        compiler_params=params(20),
        cost_estimate=cost(6e9, 4e6, 4.2e6),
        name="process",
    )(near, half, normed, other, stay(link_update_matrix), mesh_to_grid_matrix.T)
    decoded, *parts[1:] = lax.optimization_barrier((decoded, *parts[1:]))
    decoded = lax.all_to_all(decoded, "ens", split_axis=0, concat_axis=0, tiled=True)
    decoded = decoded.reshape(members * PAD, nodes).T
    table = lax.all_to_all(
        jnp.broadcast_to(decoded[None], (spaces // 2, nodes, members * PAD)),
        "space",
        split_axis=0,
        concat_axis=0,
        tiled=True,
        axis_index_groups=[list(range(c, spaces, 2)) for c in range(2)],
    ).reshape(spaces // 2 * nodes, members * PAD)
    table_other = lax.ppermute(table, "space", [(i, i ^ 1) for i in range(spaces)])
    rows = -(-PART * (blocks + blocks // members) // 16) * 16
    slopes = pl.pallas_call(
        crps_kernel,
        out_shape=shape((members, rows, LANE), BF16),
        in_specs=[SM] * 2 + [VM] * (4 + members),
        out_specs=VM,
        scratch_shapes=[
            pltpu.VMEM((spaces * nodes, LANE), F32),
            pltpu.VMEM((members * held + (PAD - PART) * blocks, LANE), F32),
            pltpu.VMEM((members * rows, LANE), F32),
            pltpu.VMEM((2 * LANE, LANE), F32),
            pltpu.VMEM((2 * members * PAD, LANE), F32),
        ],
        compiler_params=params(20),
        cost_estimate=cost(5e9, 6e6, 2e6),
        name="crps",
    )(
        member.astype(jnp.int32).reshape(1),
        ids,
        table,
        table_other,
        seen,
        area.reshape(blocks, LANE),
        *parts,
    )
    slopes = lax.all_to_all(slopes, "ens", split_axis=0, concat_axis=0, tiled=True)
    crps, grads = pl.pallas_call(
        unpack_kernel,
        out_shape=(shape((variables, points // members), F32), shape((variables * blocks, LANE), F32)),
        in_specs=[VM],
        out_specs=(VM, VM),
        scratch_shapes=[pltpu.VMEM((rows, LANE), F32)],
        compiler_params=params(16),
        cost_estimate=cost(1e6, 2e6),
        name="unpack",
    )(slopes)
    return crps, grads.reshape(1, variables, points)


def solution(mesh):
    return jax.shard_map(
        local,
        mesh=mesh,
        in_specs=(
            P("ens", None, "space"),
            P("space", None),
            P("space"),
            P("space", None),
            P("space", None),
            P(),
            P(),
            P(),
            P(),
            P(),
            P(),
            P(None, "space"),
            P("space"),
        ),
        out_specs=(P(None, ("space", "ens")), P("ens", None, "space")),
        check_vma=False,
    )
```

```python
import functools

import jax
import jax.numpy as jnp
from jax import lax
from jax.experimental import pallas as pl
from jax.experimental.pallas import tpu as pltpu
from jax.sharding import PartitionSpec as P

SLOTS = 192
LANE = 128
SENT = 160
PART = 13
PAD = 16
BF16, F32 = jnp.bfloat16, jnp.float32
VM = pl.BlockSpec(memory_space=pltpu.VMEM)
SM = pl.BlockSpec(memory_space=pltpu.SMEM)


HBM = pl.BlockSpec(memory_space=pltpu.HBM)


def cost(flops, moved, transcendentals=0):
    return pl.CostEstimate(flops=int(flops), bytes_accessed=int(moved), transcendentals=int(transcendentals))


def stay(array):
    return pltpu.with_memory_space_constraint(array, pltpu.HBM)


def params(mib):
    return pltpu.CompilerParams(vmem_limit_bytes=mib * 2**20)


def pack_kernel(
    core_ref, own_hbm, owner_hbm, local_hbm, slots_ref, ids_ref, *rest
):
    *parts, own_ref, owner_ref, local_ref, wide, rows, slots, flat, pos_v, pos_s, sems = rest
    loads = [
        pltpu.make_async_copy(owner_hbm, owner_ref, sems.at[0]),
        pltpu.make_async_copy(local_hbm, local_ref, sems.at[1]),
        pltpu.make_async_copy(own_hbm, own_ref, sems.at[2]),
    ]
    for load in loads:
        load.start()
    slots[...] = jnp.zeros_like(slots)
    loads[0].wait()
    loads[1].wait()
    variables = own_ref.shape[0]
    blocks = owner_ref.shape[0]
    spaces = slots.shape[0] // SLOTS
    row = lax.broadcasted_iota(jnp.int32, (LANE, 2 * LANE), 0)
    col = lax.broadcasted_iota(jnp.int32, (LANE, 2 * LANE), 1)
    before = jnp.where((row < col) | (col >= LANE), 1.0, 0.0).astype(BF16)
    names = lax.broadcasted_iota(jnp.int32, (spaces, LANE), 0)
    carry = jnp.zeros((spaces, LANE), F32)
    for j in range(blocks):
        owner = owner_ref[j : j + 1, :]
        hot = jnp.where(names == owner, 1.0, 0.0)
        counts = jnp.dot(hot.astype(BF16), before, preferred_element_type=F32)
        rank = jnp.sum(hot * (counts[:, :LANE] + carry), axis=0, keepdims=True)
        carry = carry + counts[:, LANE:]
        pos_v[j : j + 1, :] = owner * SLOTS + rank.astype(jnp.int32)
    side = jnp.where(owner_ref[...] % 2 == core_ref[0], 0, spaces // 2)
    ids_ref[...] = (side + owner_ref[...] // 2) * LANE + local_ref[...]
    copy = pltpu.make_async_copy(pos_v, pos_s, sems.at[3])
    copy.start()
    loads[2].wait()
    wide[variables:, :] = jnp.zeros((LANE - variables, wide.shape[1]), F32)
    wide[:variables, :] = own_ref[...].astype(F32)
    members = len(parts)
    for j in range(blocks):
        for low in range(0, variables, 8):
            count = min(8, variables - low)
            flat[pl.ds(low * blocks + j, count, stride=blocks), :] = wide[low : low + count, j * LANE : (j + 1) * LANE]
    flat[variables * blocks :, :] = jnp.zeros((flat.shape[0] - variables * blocks, LANE), F32)
    for d in range(members):
        first = pl.multiple_of((core_ref[1] + d) % members * (PART * blocks), 8)
        parts[d][...] = flat[pl.ds(first, parts[d].shape[0]), :].astype(BF16)
    for j in range(blocks):
        wide[variables : variables + 1, j * LANE : (j + 1) * LANE] = local_ref[j : j + 1, :].astype(F32)
    for j in range(blocks):
        rows[j * LANE : (j + 1) * LANE, :] = wide[:, j * LANE : (j + 1) * LANE].T
    copy.wait()

    def place(j, _):
        for i in range(0, LANE, 16):
            base = pl.multiple_of(j * LANE + i, 16)
            held = [rows[pl.ds(base + k, 1), :] for k in range(16)]
            for k in range(16):
                slots[pl.ds(pos_s[j, i + k], 1), :] = held[k]
        return 0

    lax.fori_loop(0, blocks, place, 0)
    used = variables + 1
    spare = LANE - used
    more = SLOTS - SENT
    lanes = lax.broadcasted_iota(jnp.int32, (more, LANE), 1)
    for o in range(spaces):
        beyond = slots[o * SLOTS + SENT : (o + 1) * SLOTS, :]
        for p in range(SENT // more):
            piece = slots[o * SLOTS + p * more : o * SLOTS + (p + 1) * more, :]
            if p * spare < used:
                piece = jnp.where(lanes >= used, pltpu.roll(beyond, used - p * spare, 1), piece)
            slots_ref[o * SENT + p * more : o * SENT + (p + 1) * more, :] = piece.astype(BF16)


def encode_kernel(
    slots_ref,
    embed_ref,
    latent_ref,
    gain_ref,
    sender_ref,
    normed_ref,
    source_ref,
    beyond,
    sender,
    sem,
):
    copy = pltpu.make_async_copy(sender_ref, sender, sem)
    copy.start()
    variables = embed_ref.shape[0]
    width = embed_ref.shape[1]
    chunk = 512
    half = jnp.concatenate([embed_ref[...].astype(F32) * 0.5, jnp.zeros((LANE - variables, width), F32)], axis=0).astype(BF16)
    lanes = lax.broadcasted_iota(jnp.int32, (chunk, LANE), 1).astype(F32)
    state = latent_ref[...].astype(F32)
    used = variables + 1
    spare = LANE - used
    more = SLOTS - SENT
    place = lax.broadcasted_iota(jnp.int32, (more, LANE), 1)
    for o in range(slots_ref.shape[0] // SENT):
        whole = jnp.zeros((more, LANE), F32)
        for p in range(-(-used // spare)):
            piece = slots_ref[o * SENT + p * more : o * SENT + (p + 1) * more, :].astype(F32)
            there = (place >= p * spare) & (place < (p + 1) * spare)
            whole = jnp.where(there, pltpu.roll(piece, (p * spare - used) % LANE, 1), whole)
        beyond[o * more : (o + 1) * more, :] = whole.astype(BF16)
    whole = slots_ref.shape[0] // chunk
    for c in range(whole + beyond.shape[0] // chunk):
        if c < whole:
            x = slots_ref[c * chunk : (c + 1) * chunk, :]
        else:
            x = beyond[(c - whole) * chunk : (c - whole + 1) * chunk, :]
        h = jnp.dot(x, half, preferred_element_type=F32)
        act = (h + h * jnp.tanh(h)).astype(BF16)
        node = x[:, variables : variables + 1].astype(F32)
        hot = jnp.where(node == lanes, 1.0, 0.0).astype(BF16)
        state = state + lax.dot_general(hot, act, (((0,), (0,)), ((), ())), preferred_element_type=F32)
    centred = state - jnp.mean(state, axis=-1, keepdims=True)
    spread = jnp.mean(centred * centred, axis=-1, keepdims=True)
    normed = (centred * lax.rsqrt(spread + 1e-05) * gain_ref[...]).astype(BF16)
    normed_ref[...] = normed
    copy.wait()
    source_ref[...] = jnp.dot(normed, sender[...], preferred_element_type=F32).astype(BF16)


def near_kernel(
    member_ref,
    near_ref,
    normed_ref,
    sibling_ref,
    own_ref,
    receiver_hbm,
    observed_hbm,
    link_hbm,
    half_ref,
    seen_ref,
    link_ref,
    receiver,
    observed,
    beside,
    sems,
):
    loads = [
        pltpu.make_async_copy(receiver_hbm, receiver, sems.at[0]),
        pltpu.make_async_copy(observed_hbm, observed, sems.at[1]),
        pltpu.make_async_copy(link_hbm, link_ref, sems.at[2]),
    ]
    for load in loads:
        load.start()
    nodes, fanout = near_ref.shape
    group = 4
    beside[:nodes, :] = sibling_ref[...]
    beside[nodes:, :] = own_ref[...]
    lanes = lax.broadcasted_iota(jnp.int32, (nodes, 2 * nodes), 1)
    loads[0].wait()
    query = 0.5 * jnp.dot(normed_ref[...], receiver[...], preferred_element_type=F32)
    for g in range(0, fanout, group):
        hot = jnp.concatenate(
            [jnp.where(near_ref[:, k : k + 1] == lanes, 0.5, 0.0) for k in range(g, g + group)], axis=0
        ).astype(BF16)
        picked = jnp.dot(hot, beside[...], preferred_element_type=F32)
        half_ref[g * nodes : (g + group) * nodes, :] = picked + jnp.concatenate([query] * group, axis=0)
    loads[1].wait()
    variables = observed.shape[0]
    for c in range(-(-variables // PART)):

        @pl.when(member_ref[0] == c)
        def _():
            count = min(PART, variables - c * PART)
            seen_ref[...] = jnp.zeros_like(seen_ref)
            seen_ref[:count, :] = observed[c * PART : c * PART + count, :]

    loads[2].wait()


def process_kernel(
    near_ref, half_ref, normed_ref, other_ref, link_ref, decode_ref, out_ref, edges, total, spaced
):
    nodes, fanout = near_ref.shape
    variables = decode_ref.shape[0]
    group = 4
    lanes = lax.broadcasted_iota(jnp.int32, (nodes, nodes), 1) + 2 * nodes
    for g in range(0, fanout, group):
        hot = jnp.concatenate(
            [jnp.where(near_ref[:, k : k + 1] == lanes, 0.5, 0.0) for k in range(g, g + group)], axis=0
        ).astype(BF16)
        h = half_ref[g * nodes : (g + group) * nodes, :] + jnp.dot(hot, other_ref[...], preferred_element_type=F32)
        edges[g * nodes : (g + group) * nodes, :] = (h + h * jnp.tanh(h)).astype(BF16)
    for g in range(0, fanout, group):
        z = jnp.dot(edges[g * nodes : (g + group) * nodes, :], link_ref[...], preferred_element_type=F32)
        z = z + z * jnp.tanh(0.5 * z)
        part = sum(z[k * nodes : (k + 1) * nodes] for k in range(group))
        if g == 0:
            total[...] = part
        else:
            total[...] += part
    updated = (normed_ref[...].astype(F32) + total[...] * (0.5 / fanout)).astype(BF16)
    decoded = lax.dot_general(decode_ref[...], updated, (((1,), (1,)), ((), ())), preferred_element_type=F32)
    spaced[...] = jnp.zeros_like(spaced)
    for c in range(out_ref.shape[0]):
        held = min(PART, variables - c * PART)
        spaced[c * PAD : c * PAD + held, :] = decoded[c * PART : c * PART + held, :]
    for c in range(out_ref.shape[0]):
        out_ref[c] = spaced[c * PAD : (c + 1) * PAD, :].astype(BF16)


def crps_kernel(member_ref, ids_ref, table_ref, other_ref, seen, area_ref, *rest):
    *parts, out_ref, table, states, slopes, picked, held = rest
    members = len(parts)
    names = [(member_ref[0] + members - d) % members for d in range(members)]
    blocks = ids_ref.shape[0]
    per_member = blocks // members
    rows = out_ref.shape[1]
    half = table_ref.shape[0]
    table[:half, :] = table_ref[...].astype(F32)
    table[half:, :] = other_ref[...].astype(F32)
    size = parts[0].shape[0]
    for d in range(members):
        states[d * size : (d + 1) * size, :] = parts[d][...].astype(F32)
    states[members * size :, :] = jnp.zeros((states.shape[0] - members * size, LANE), F32)
    for m in range(members):
        slopes[m * rows + rows - 8 : (m + 1) * rows, :] = jnp.zeros((8, LANE), F32)
    def fetch(j, turn):
        for i in range(0, LANE, 16):
            row = [table[pl.ds(ids_ref[j, i + k], 1), :] for k in range(16)]
            for k in range(16):
                picked[turn * LANE + i + k : turn * LANE + i + k + 1, :] = row[k]

    def score(j, turn):
        here = pl.ds(pl.multiple_of(j * LANE, LANE), LANE)
        held[turn * LANE : (turn + 1) * LANE, :] = picked[turn * LANE : (turn + 1) * LANE, :].T
        area = area_ref[pl.ds(j, 1), :]
        spare = j // per_member * rows + PART * blocks + j % per_member
        for low in range(0, PAD, 8):
            count = min(8, PART - low)
            start = turn * LANE + low
            f = [
                held[pl.ds(pl.multiple_of(start + names[m] * PAD, 8), 8), :] + states[pl.ds(m * size + low * blocks + j, 8, stride=blocks), :]
                for m in range(members)
            ]
            obs = seen[low : low + 8, here]
            slope = [None] * members
            pairs = None
            for a in range(members):
                for b in range(a + 1, members):
                    d = f[a] - f[b]
                    q = d * d + 0.01
                    r = lax.rsqrt(q)
                    t = d * r
                    pairs = q * r if pairs is None else pairs + q * r
                    slope[a] = t if slope[a] is None else slope[a] + t
                    slope[b] = -t if slope[b] is None else slope[b] - t
            near = None
            for m in range(members):
                miss = f[m] - obs
                q = miss * miss + 0.01
                r = lax.rsqrt(q)
                near = q * r if near is None else near + q * r
                value = area * (miss * r - slope[m] * (1.0 / (members - 1)))
                slopes[pl.ds(names[m] * rows + low * blocks + j, count, stride=blocks), :] = value[:count]
            pairs = (2.0 * pairs + 0.1 * members) * (1.0 / (2.0 * members * (members - 1)))
            value = area * (near * (1.0 / members) - pairs)
            slopes[pl.ds(spare + low * per_member, count, stride=per_member), :] = value[:count]

    fetch(0, 0)

    def two(i, _):
        fetch(2 * i + 1, 1)
        score(2 * i, 0)
        fetch(jnp.minimum(2 * i + 2, blocks - 1), 0)
        score(2 * i + 1, 1)
        return 0

    lax.fori_loop(0, blocks // 2, two, 0)
    for m in range(members):
        out_ref[m] = slopes[m * rows : (m + 1) * rows, :].astype(BF16)


def unpack_kernel(got_ref, crps_ref, grads_ref, wide):
    variables, points = crps_ref.shape
    parts = got_ref.shape[0]
    per_part = points // LANE
    blocks = parts * per_part
    for c in range(parts):
        wide[...] = got_ref[c].astype(F32)
        held = min(PART, variables - c * PART)
        grads_ref[c * PART * blocks : (c * PART + held) * blocks, :] = wide[: held * blocks, :]
        for j in range(per_part):
            crps_ref[c * PART : c * PART + held, j * LANE : (j + 1) * LANE] = wide[
                pl.ds(PART * blocks + j, held, stride=per_part), :
            ]


def local(
    initial_states,
    owner,
    node_local,
    adjacent_vertex_ids,
    vertex_latents,
    norm_factor,
    grid_to_mesh_matrix,
    receiver_matrix,
    sender_matrix,
    link_update_matrix,
    mesh_to_grid_matrix,
    observed,
    area,
):
    spaces = lax.axis_size("space")
    members = lax.axis_size("ens")
    variables, points = initial_states.shape[1:]
    nodes, width = vertex_latents.shape
    fanout = adjacent_vertex_ids.shape[1]
    blocks = points // LANE
    shape = jax.ShapeDtypeStruct
    place = lax.axis_index("space")
    core = place % 2
    member = lax.axis_index("ens")
    held = -(-PART * blocks // 16) * 16
    slots, ids, *parts = pl.pallas_call(
        pack_kernel,
        out_shape=(
            shape((spaces * SENT, LANE), BF16),
            shape((blocks, LANE), jnp.int32),
            *[shape((held, LANE), BF16)] * members,
        ),
        in_specs=[SM] + [HBM] * 3,
        out_specs=(VM,) * (2 + members),
        scratch_shapes=[
            pltpu.VMEM((variables, points), BF16),
            pltpu.VMEM((blocks, LANE), jnp.int32),
            pltpu.VMEM((blocks, LANE), jnp.int32),
            pltpu.VMEM((LANE, points), F32),
            pltpu.VMEM((points, LANE), F32),
            pltpu.VMEM((spaces * SLOTS, LANE), F32),
            pltpu.VMEM(((members - 1) * PART * blocks + held, LANE), F32),
            pltpu.VMEM((blocks, LANE), jnp.int32),
            pltpu.SMEM((blocks, LANE), jnp.int32),
            pltpu.SemaphoreType.DMA((4,)),
        ],
        compiler_params=params(16),
        cost_estimate=cost(1.5e8, 8e6),
        name="pack",
    )(
        jnp.stack([core, member]).astype(jnp.int32),
        stay(initial_states[0]),
        stay(owner.reshape(blocks, LANE)),
        stay(node_local.reshape(blocks, LANE)),
    )
    got = lax.all_to_all(slots.reshape(spaces, SENT, LANE), "space", split_axis=0, concat_axis=0, tiled=True)
    for d in (3, 5, 2, 6, 1, 7, 4):
        parts[d] = lax.ppermute(parts[d], "ens", [(i, (i + d) % members) for i in range(members)])
    soon = (3, 5)
    got, *moved = lax.optimization_barrier((got, *[parts[d] for d in soon]))
    for d, part in zip(soon, moved):
        parts[d] = part
    normed, source = pl.pallas_call(
        encode_kernel,
        out_shape=(shape((nodes, width), BF16), shape((nodes, width), BF16)),
        in_specs=[VM] * 4 + [HBM],
        out_specs=(VM,) * 2,
        scratch_shapes=[
            pltpu.VMEM((spaces * (SLOTS - SENT), LANE), BF16),
            pltpu.VMEM((width, width), BF16),
            pltpu.SemaphoreType.DMA,
        ],
        compiler_params=params(20),
        cost_estimate=cost(4e9, 8e6, 6.3e6),
        name="encode",
    )(
        got.reshape(spaces * SENT, LANE),
        grid_to_mesh_matrix,
        vertex_latents,
        norm_factor.reshape(1, width),
        stay(sender_matrix),
    )
    source, *moved = lax.optimization_barrier((source, *[parts[d] for d in (2, 6, 1, 7, 4)]))
    for d, part in zip((2, 6, 1, 7, 4), moved):
        parts[d] = part
    sibling = lax.ppermute(source, "space", [(i, i ^ 1) for i in range(spaces)])
    other = lax.ppermute(source, "space", [(i, (i + 2 * (i % 2) - 1) % spaces) for i in range(spaces)])
    home = adjacent_vertex_ids // nodes
    slab = jnp.where(home == place, 1, jnp.where(home == place + 1 - 2 * core, 0, 2))
    near = slab * nodes + adjacent_vertex_ids % nodes
    half, seen, link = pl.pallas_call(
        near_kernel,
        out_shape=(shape((fanout * nodes, width), F32), shape((PAD, points), F32), shape((width, width), BF16)),
        in_specs=[SM] + [VM] * 4 + [HBM] * 3,
        out_specs=(VM,) * 3,
        scratch_shapes=[
            pltpu.VMEM((width, width), BF16),
            pltpu.VMEM((variables, points), F32),
            pltpu.VMEM((2 * nodes, width), BF16),
            pltpu.SemaphoreType.DMA((3,)),
        ],
        compiler_params=params(16),
        cost_estimate=cost(2e9, 4e6),
        name="near",
    )(
        member.astype(jnp.int32).reshape(1),
        near,
        normed,
        sibling,
        source,
        stay(receiver_matrix),
        stay(observed),
        stay(link_update_matrix),
    )
    decoded = pl.pallas_call(
        process_kernel,
        out_shape=shape((members, PAD, nodes), BF16),
        in_specs=[VM] * 6,
        out_specs=VM,
        scratch_shapes=[
            pltpu.VMEM((fanout * nodes, width), BF16),
            pltpu.VMEM((nodes, width), F32),
            pltpu.VMEM((members * PAD, nodes), F32),
        ],
        compiler_params=params(20),
        cost_estimate=cost(6e9, 4e6, 4.2e6),
        name="process",
    )(near, half, normed, other, link, mesh_to_grid_matrix.T)
    decoded, *parts[1:] = lax.optimization_barrier((decoded, *parts[1:]))
    decoded = lax.all_to_all(decoded, "ens", split_axis=0, concat_axis=0, tiled=True)
    decoded = decoded.reshape(members * PAD, nodes).T
    table = lax.all_to_all(
        jnp.broadcast_to(decoded[None], (spaces // 2, nodes, members * PAD)),
        "space",
        split_axis=0,
        concat_axis=0,
        tiled=True,
        axis_index_groups=[list(range(c, spaces, 2)) for c in range(2)],
    ).reshape(spaces // 2 * nodes, members * PAD)
    table_other = lax.ppermute(table, "space", [(i, i ^ 1) for i in range(spaces)])
    rows = -(-PART * (blocks + blocks // members) // 16) * 16
    slopes = pl.pallas_call(
        crps_kernel,
        out_shape=shape((members, rows, LANE), BF16),
        in_specs=[SM] * 2 + [VM] * (4 + members),
        out_specs=VM,
        scratch_shapes=[
            pltpu.VMEM((spaces * nodes, LANE), F32),
            pltpu.VMEM((members * held + (PAD - PART) * blocks, LANE), F32),
            pltpu.VMEM((members * rows, LANE), F32),
            pltpu.VMEM((2 * LANE, LANE), F32),
            pltpu.VMEM((2 * members * PAD, LANE), F32),
        ],
        compiler_params=params(20),
        cost_estimate=cost(5e9, 6e6, 2e6),
        name="crps",
    )(
        member.astype(jnp.int32).reshape(1),
        ids,
        table,
        table_other,
        seen,
        area.reshape(blocks, LANE),
        *parts,
    )
    slopes = lax.all_to_all(slopes, "ens", split_axis=0, concat_axis=0, tiled=True)
    crps, grads = pl.pallas_call(
        unpack_kernel,
        out_shape=(shape((variables, points // members), F32), shape((variables * blocks, LANE), F32)),
        in_specs=[VM],
        out_specs=(VM, VM),
        scratch_shapes=[pltpu.VMEM((rows, LANE), F32)],
        compiler_params=params(16),
        cost_estimate=cost(1e6, 2e6),
        name="unpack",
    )(slopes)
    return crps, grads.reshape(1, variables, points)


def solution(mesh):
    return jax.shard_map(
        local,
        mesh=mesh,
        in_specs=(
            P("ens", None, "space"),
            P("space", None),
            P("space"),
            P("space", None),
            P("space", None),
            P(),
            P(),
            P(),
            P(),
            P(),
            P(),
            P(None, "space"),
            P("space"),
        ),
        out_specs=(P(None, ("space", "ens")), P("ens", None, "space")),
        check_vma=False,
    )
```

```python
import functools

import jax
import jax.numpy as jnp
from jax import lax
from jax.experimental import pallas as pl
from jax.experimental.pallas import tpu as pltpu
from jax.sharding import PartitionSpec as P

SLOTS = 192
LANE = 128
SENT = 160
PART = 13
PAD = 16
BF16, F32 = jnp.bfloat16, jnp.float32
VM = pl.BlockSpec(memory_space=pltpu.VMEM)
SM = pl.BlockSpec(memory_space=pltpu.SMEM)


HBM = pl.BlockSpec(memory_space=pltpu.HBM)


def cost(flops, moved, transcendentals=0):
    return pl.CostEstimate(flops=int(flops), bytes_accessed=int(moved), transcendentals=int(transcendentals))


def stay(array):
    return pltpu.with_memory_space_constraint(array, pltpu.HBM)


def params(mib):
    return pltpu.CompilerParams(vmem_limit_bytes=mib * 2**20)


def pack_kernel(
    core_ref, own_hbm, owner_hbm, local_hbm, slots_ref, ids_ref, *rest
):
    *parts, own_ref, owner_ref, local_ref, wide, rows, slots, flat, pos_v, pos_s, sems = rest
    loads = [
        pltpu.make_async_copy(owner_hbm, owner_ref, sems.at[0]),
        pltpu.make_async_copy(local_hbm, local_ref, sems.at[1]),
        pltpu.make_async_copy(own_hbm, own_ref, sems.at[2]),
    ]
    for load in loads:
        load.start()
    slots[...] = jnp.zeros_like(slots)
    loads[0].wait()
    loads[1].wait()
    variables = own_ref.shape[0]
    blocks = owner_ref.shape[0]
    spaces = slots.shape[0] // SLOTS
    row = lax.broadcasted_iota(jnp.int32, (LANE, 2 * LANE), 0)
    col = lax.broadcasted_iota(jnp.int32, (LANE, 2 * LANE), 1)
    before = jnp.where((row < col) | (col >= LANE), 1.0, 0.0).astype(BF16)
    names = lax.broadcasted_iota(jnp.int32, (spaces, LANE), 0)
    carry = jnp.zeros((spaces, LANE), F32)
    for j in range(blocks):
        owner = owner_ref[j : j + 1, :]
        hot = jnp.where(names == owner, 1.0, 0.0)
        counts = jnp.dot(hot.astype(BF16), before, preferred_element_type=F32)
        rank = jnp.sum(hot * (counts[:, :LANE] + carry), axis=0, keepdims=True)
        carry = carry + counts[:, LANE:]
        pos_v[j : j + 1, :] = owner * SLOTS + rank.astype(jnp.int32)
    side = jnp.where(owner_ref[...] % 2 == core_ref[0], 0, spaces // 2)
    ids_ref[...] = (side + owner_ref[...] // 2) * LANE + local_ref[...]
    copy = pltpu.make_async_copy(pos_v, pos_s, sems.at[3])
    copy.start()
    loads[2].wait()
    wide[variables:, :] = jnp.zeros((LANE - variables, wide.shape[1]), F32)
    wide[:variables, :] = own_ref[...].astype(F32)
    members = len(parts)
    for j in range(blocks):
        for low in range(0, variables, 8):
            count = min(8, variables - low)
            flat[pl.ds(low * blocks + j, count, stride=blocks), :] = wide[low : low + count, j * LANE : (j + 1) * LANE]
    flat[variables * blocks :, :] = jnp.zeros((flat.shape[0] - variables * blocks, LANE), F32)
    for d in range(members):
        first = pl.multiple_of((core_ref[1] + d) % members * (PART * blocks), 8)
        parts[d][...] = flat[pl.ds(first, parts[d].shape[0]), :].astype(BF16)
    for j in range(blocks):
        wide[variables : variables + 1, j * LANE : (j + 1) * LANE] = local_ref[j : j + 1, :].astype(F32)
    for j in range(blocks):
        rows[j * LANE : (j + 1) * LANE, :] = wide[:, j * LANE : (j + 1) * LANE].T
    copy.wait()

    def place(j, _):
        for i in range(0, LANE, 16):
            base = pl.multiple_of(j * LANE + i, 16)
            held = [rows[pl.ds(base + k, 1), :] for k in range(16)]
            for k in range(16):
                slots[pl.ds(pos_s[j, i + k], 1), :] = held[k]
        return 0

    lax.fori_loop(0, blocks, place, 0)
    used = variables + 1
    spare = LANE - used
    more = SLOTS - SENT
    lanes = lax.broadcasted_iota(jnp.int32, (more, LANE), 1)
    for o in range(spaces):
        beyond = slots[o * SLOTS + SENT : (o + 1) * SLOTS, :]
        for p in range(SENT // more):
            piece = slots[o * SLOTS + p * more : o * SLOTS + (p + 1) * more, :]
            if p * spare < used:
                piece = jnp.where(lanes >= used, pltpu.roll(beyond, used - p * spare, 1), piece)
            slots_ref[o * SENT + p * more : o * SENT + (p + 1) * more, :] = piece.astype(BF16)


def encode_kernel(
    slots_ref,
    embed_ref,
    latent_ref,
    gain_ref,
    sender_ref,
    normed_ref,
    source_ref,
    beyond,
    sender,
    sem,
):
    copy = pltpu.make_async_copy(sender_ref, sender, sem)
    copy.start()
    variables = embed_ref.shape[0]
    width = embed_ref.shape[1]
    chunk = 512
    half = jnp.concatenate([embed_ref[...].astype(F32) * 0.5, jnp.zeros((LANE - variables, width), F32)], axis=0).astype(BF16)
    lanes = lax.broadcasted_iota(jnp.int32, (chunk, LANE), 1).astype(F32)
    state = latent_ref[...].astype(F32)
    used = variables + 1
    spare = LANE - used
    more = SLOTS - SENT
    place = lax.broadcasted_iota(jnp.int32, (more, LANE), 1)
    for o in range(slots_ref.shape[0] // SENT):
        whole = jnp.zeros((more, LANE), F32)
        for p in range(-(-used // spare)):
            piece = slots_ref[o * SENT + p * more : o * SENT + (p + 1) * more, :].astype(F32)
            there = (place >= p * spare) & (place < (p + 1) * spare)
            whole = jnp.where(there, pltpu.roll(piece, (p * spare - used) % LANE, 1), whole)
        beyond[o * more : (o + 1) * more, :] = whole.astype(BF16)
    whole = slots_ref.shape[0] // chunk
    for c in range(whole + beyond.shape[0] // chunk):
        if c < whole:
            x = slots_ref[c * chunk : (c + 1) * chunk, :]
        else:
            x = beyond[(c - whole) * chunk : (c - whole + 1) * chunk, :]
        h = jnp.dot(x, half, preferred_element_type=F32)
        act = (h + h * jnp.tanh(h)).astype(BF16)
        node = x[:, variables : variables + 1].astype(F32)
        hot = jnp.where(node == lanes, 1.0, 0.0).astype(BF16)
        state = state + lax.dot_general(hot, act, (((0,), (0,)), ((), ())), preferred_element_type=F32)
    centred = state - jnp.mean(state, axis=-1, keepdims=True)
    spread = jnp.mean(centred * centred, axis=-1, keepdims=True)
    normed = (centred * lax.rsqrt(spread + 1e-05) * gain_ref[...]).astype(BF16)
    normed_ref[...] = normed
    copy.wait()
    source_ref[...] = jnp.dot(normed, sender[...], preferred_element_type=F32).astype(BF16)


def near_kernel(
    member_ref,
    near_ref,
    normed_ref,
    sibling_ref,
    own_ref,
    receiver_hbm,
    observed_hbm,
    link_hbm,
    half_ref,
    seen_ref,
    link_ref,
    receiver,
    observed,
    beside,
    sems,
):
    loads = [
        pltpu.make_async_copy(receiver_hbm, receiver, sems.at[0]),
        pltpu.make_async_copy(observed_hbm, observed, sems.at[1]),
        pltpu.make_async_copy(link_hbm, link_ref, sems.at[2]),
    ]
    for load in loads:
        load.start()
    nodes, fanout = near_ref.shape
    group = 4
    beside[:nodes, :] = sibling_ref[...]
    beside[nodes:, :] = own_ref[...]
    lanes = lax.broadcasted_iota(jnp.int32, (nodes, 2 * nodes), 1)
    loads[0].wait()
    query = 0.5 * jnp.dot(normed_ref[...], receiver[...], preferred_element_type=F32)
    for g in range(0, fanout, group):
        hot = jnp.concatenate(
            [jnp.where(near_ref[:, k : k + 1] == lanes, 0.5, 0.0) for k in range(g, g + group)], axis=0
        ).astype(BF16)
        picked = jnp.dot(hot, beside[...], preferred_element_type=F32)
        half_ref[g * nodes : (g + group) * nodes, :] = picked + jnp.concatenate([query] * group, axis=0)
    loads[1].wait()
    variables = observed.shape[0]
    for c in range(-(-variables // PART)):

        @pl.when(member_ref[0] == c)
        def _():
            count = min(PART, variables - c * PART)
            seen_ref[...] = jnp.zeros_like(seen_ref)
            seen_ref[:count, :] = observed[c * PART : c * PART + count, :]

    loads[2].wait()


def process_kernel(
    near_ref, half_ref, normed_ref, other_ref, link_ref, decode_ref, out_ref, edges, total, spaced
):
    nodes, fanout = near_ref.shape
    variables = decode_ref.shape[0]
    group = 4
    lanes = lax.broadcasted_iota(jnp.int32, (nodes, nodes), 1) + 2 * nodes
    for g in range(0, fanout, group):
        hot = jnp.concatenate(
            [jnp.where(near_ref[:, k : k + 1] == lanes, 0.5, 0.0) for k in range(g, g + group)], axis=0
        ).astype(BF16)
        h = half_ref[g * nodes : (g + group) * nodes, :] + jnp.dot(hot, other_ref[...], preferred_element_type=F32)
        edges[g * nodes : (g + group) * nodes, :] = (h + h * jnp.tanh(h)).astype(BF16)
    for g in range(0, fanout, group):
        z = jnp.dot(edges[g * nodes : (g + group) * nodes, :], link_ref[...], preferred_element_type=F32)
        z = z + z * jnp.tanh(0.5 * z)
        part = sum(z[k * nodes : (k + 1) * nodes] for k in range(group))
        if g == 0:
            total[...] = part
        else:
            total[...] += part
    updated = (normed_ref[...].astype(F32) + total[...] * (0.5 / fanout)).astype(BF16)
    decoded = lax.dot_general(decode_ref[...], updated, (((1,), (1,)), ((), ())), preferred_element_type=F32)
    spaced[...] = jnp.zeros_like(spaced)
    for c in range(out_ref.shape[0]):
        held = min(PART, variables - c * PART)
        spaced[c * PAD : c * PAD + held, :] = decoded[c * PART : c * PART + held, :]
    for c in range(out_ref.shape[0]):
        out_ref[c] = spaced[c * PAD : (c + 1) * PAD, :].astype(BF16)


def crps_kernel(member_ref, ids_ref, table_ref, other_ref, seen, area_ref, *rest):
    *arrays, table, states, slopes, picked, held = rest
    members = len(arrays) // 2
    parts, outs = arrays[:members], arrays[members:]
    names = [(member_ref[0] + members - d) % members for d in range(members)]
    blocks = ids_ref.shape[0]
    per_member = blocks // members
    rows = outs[0].shape[0]
    half = table_ref.shape[0]
    table[:half, :] = table_ref[...].astype(F32)
    table[half:, :] = other_ref[...].astype(F32)
    size = parts[0].shape[0]
    for d in range(members):
        states[d * size : (d + 1) * size, :] = parts[d][...].astype(F32)
    states[members * size :, :] = jnp.zeros((states.shape[0] - members * size, LANE), F32)
    for m in range(members):
        slopes[m * rows + rows - 8 : (m + 1) * rows, :] = jnp.zeros((8, LANE), F32)
    def fetch(j, turn):
        for i in range(0, LANE, 16):
            row = [table[pl.ds(ids_ref[j, i + k], 1), :] for k in range(16)]
            for k in range(16):
                picked[turn * LANE + i + k : turn * LANE + i + k + 1, :] = row[k]

    def score(j, turn):
        here = pl.ds(pl.multiple_of(j * LANE, LANE), LANE)
        held[turn * LANE : (turn + 1) * LANE, :] = picked[turn * LANE : (turn + 1) * LANE, :].T
        area = area_ref[pl.ds(j, 1), :]
        spare = (member_ref[0] + members - j // per_member) % members * rows + PART * blocks + j % per_member
        for low in range(0, PAD, 8):
            count = min(8, PART - low)
            start = turn * LANE + low
            f = [
                held[pl.ds(pl.multiple_of(start + names[m] * PAD, 8), 8), :] + states[pl.ds(m * size + low * blocks + j, 8, stride=blocks), :]
                for m in range(members)
            ]
            obs = seen[low : low + 8, here]
            slope = [None] * members
            pairs = None
            for a in range(members):
                for b in range(a + 1, members):
                    d = f[a] - f[b]
                    q = d * d + 0.01
                    r = lax.rsqrt(q)
                    t = d * r
                    pairs = q * r if pairs is None else pairs + q * r
                    slope[a] = t if slope[a] is None else slope[a] + t
                    slope[b] = -t if slope[b] is None else slope[b] - t
            near = None
            for m in range(members):
                miss = f[m] - obs
                q = miss * miss + 0.01
                r = lax.rsqrt(q)
                near = q * r if near is None else near + q * r
                value = area * (miss * r - slope[m] * (1.0 / (members - 1)))
                slopes[pl.ds(m * rows + low * blocks + j, count, stride=blocks), :] = value[:count]
            pairs = (2.0 * pairs + 0.1 * members) * (1.0 / (2.0 * members * (members - 1)))
            value = area * (near * (1.0 / members) - pairs)
            slopes[pl.ds(spare + low * per_member, count, stride=per_member), :] = value[:count]

    fetch(0, 0)

    def two(i, _):
        fetch(2 * i + 1, 1)
        score(2 * i, 0)
        fetch(jnp.minimum(2 * i + 2, blocks - 1), 0)
        score(2 * i + 1, 1)
        return 0

    lax.fori_loop(0, blocks // 2, two, 0)
    for m in range(members):
        outs[m][...] = slopes[m * rows : (m + 1) * rows, :].astype(BF16)


def unpack_kernel(member_ref, *rest):
    *got, crps_ref, grads_ref, wide, scores = rest
    variables, points = crps_ref.shape
    parts = len(got)
    per_part = points // LANE
    blocks = parts * per_part
    least = variables - (parts - 1) * PART
    size = parts * PART
    for d in range(parts):
        part = (member_ref[0] + d) % parts
        wide[...] = got[d][...].astype(F32)
        first = pl.multiple_of(part * (PART * blocks), 8)
        grads_ref[pl.ds(first, least * blocks), :] = wide[: least * blocks, :]

        @pl.when(part < parts - 1)
        def _():
            grads_ref[pl.ds(first + least * blocks, (PART - least) * blocks), :] = wide[least * blocks : PART * blocks, :]

        for v in range(PART):
            for j in range(per_part):
                row = PART * blocks + v * per_part + j
                scores[pl.ds(j * size + part * PART + v, 1), :] = wide[row : row + 1, :]
    for j in range(per_part):
        crps_ref[:, j * LANE : (j + 1) * LANE] = scores[j * size : j * size + variables, :]


def local(
    initial_states,
    owner,
    node_local,
    adjacent_vertex_ids,
    vertex_latents,
    norm_factor,
    grid_to_mesh_matrix,
    receiver_matrix,
    sender_matrix,
    link_update_matrix,
    mesh_to_grid_matrix,
    observed,
    area,
):
    spaces = lax.axis_size("space")
    members = lax.axis_size("ens")
    variables, points = initial_states.shape[1:]
    nodes, width = vertex_latents.shape
    fanout = adjacent_vertex_ids.shape[1]
    blocks = points // LANE
    shape = jax.ShapeDtypeStruct
    place = lax.axis_index("space")
    core = place % 2
    member = lax.axis_index("ens")
    held = -(-PART * blocks // 16) * 16
    slots, ids, *parts = pl.pallas_call(
        pack_kernel,
        out_shape=(
            shape((spaces * SENT, LANE), BF16),
            shape((blocks, LANE), jnp.int32),
            *[shape((held, LANE), BF16)] * members,
        ),
        in_specs=[SM] + [HBM] * 3,
        out_specs=(VM,) * (2 + members),
        scratch_shapes=[
            pltpu.VMEM((variables, points), BF16),
            pltpu.VMEM((blocks, LANE), jnp.int32),
            pltpu.VMEM((blocks, LANE), jnp.int32),
            pltpu.VMEM((LANE, points), F32),
            pltpu.VMEM((points, LANE), F32),
            pltpu.VMEM((spaces * SLOTS, LANE), F32),
            pltpu.VMEM(((members - 1) * PART * blocks + held, LANE), F32),
            pltpu.VMEM((blocks, LANE), jnp.int32),
            pltpu.SMEM((blocks, LANE), jnp.int32),
            pltpu.SemaphoreType.DMA((4,)),
        ],
        compiler_params=params(16),
        cost_estimate=cost(1.5e8, 8e6),
        name="pack",
    )(
        jnp.stack([core, member]).astype(jnp.int32),
        stay(initial_states[0]),
        stay(owner.reshape(blocks, LANE)),
        stay(node_local.reshape(blocks, LANE)),
    )
    got = lax.all_to_all(slots.reshape(spaces, SENT, LANE), "space", split_axis=0, concat_axis=0, tiled=True)
    for d in (3, 5, 2, 6, 1, 7, 4):
        parts[d] = lax.ppermute(parts[d], "ens", [(i, (i + d) % members) for i in range(members)])
    soon = (3, 5)
    got, *moved = lax.optimization_barrier((got, *[parts[d] for d in soon]))
    for d, part in zip(soon, moved):
        parts[d] = part
    normed, source = pl.pallas_call(
        encode_kernel,
        out_shape=(shape((nodes, width), BF16), shape((nodes, width), BF16)),
        in_specs=[VM] * 4 + [HBM],
        out_specs=(VM,) * 2,
        scratch_shapes=[
            pltpu.VMEM((spaces * (SLOTS - SENT), LANE), BF16),
            pltpu.VMEM((width, width), BF16),
            pltpu.SemaphoreType.DMA,
        ],
        compiler_params=params(20),
        cost_estimate=cost(4e9, 8e6, 6.3e6),
        name="encode",
    )(
        got.reshape(spaces * SENT, LANE),
        grid_to_mesh_matrix,
        vertex_latents,
        norm_factor.reshape(1, width),
        stay(sender_matrix),
    )
    source, *moved = lax.optimization_barrier((source, *[parts[d] for d in (2, 6, 1, 7, 4)]))
    for d, part in zip((2, 6, 1, 7, 4), moved):
        parts[d] = part
    sibling = lax.ppermute(source, "space", [(i, i ^ 1) for i in range(spaces)])
    other = lax.ppermute(source, "space", [(i, (i + 2 * (i % 2) - 1) % spaces) for i in range(spaces)])
    home = adjacent_vertex_ids // nodes
    slab = jnp.where(home == place, 1, jnp.where(home == place + 1 - 2 * core, 0, 2))
    near = slab * nodes + adjacent_vertex_ids % nodes
    half, seen, link = pl.pallas_call(
        near_kernel,
        out_shape=(shape((fanout * nodes, width), F32), shape((PAD, points), F32), shape((width, width), BF16)),
        in_specs=[SM] + [VM] * 4 + [HBM] * 3,
        out_specs=(VM,) * 3,
        scratch_shapes=[
            pltpu.VMEM((width, width), BF16),
            pltpu.VMEM((variables, points), F32),
            pltpu.VMEM((2 * nodes, width), BF16),
            pltpu.SemaphoreType.DMA((3,)),
        ],
        compiler_params=params(16),
        cost_estimate=cost(2e9, 4e6),
        name="near",
    )(
        member.astype(jnp.int32).reshape(1),
        near,
        normed,
        sibling,
        source,
        stay(receiver_matrix),
        stay(observed),
        stay(link_update_matrix),
    )
    decoded = pl.pallas_call(
        process_kernel,
        out_shape=shape((members, PAD, nodes), BF16),
        in_specs=[VM] * 6,
        out_specs=VM,
        scratch_shapes=[
            pltpu.VMEM((fanout * nodes, width), BF16),
            pltpu.VMEM((nodes, width), F32),
            pltpu.VMEM((members * PAD, nodes), F32),
        ],
        compiler_params=params(20),
        cost_estimate=cost(6e9, 4e6, 4.2e6),
        name="process",
    )(near, half, normed, other, link, mesh_to_grid_matrix.T)
    decoded, *parts[1:] = lax.optimization_barrier((decoded, *parts[1:]))
    decoded = lax.all_to_all(decoded, "ens", split_axis=0, concat_axis=0, tiled=True)
    decoded = decoded.reshape(members * PAD, nodes).T
    table = lax.all_to_all(
        jnp.broadcast_to(decoded[None], (spaces // 2, nodes, members * PAD)),
        "space",
        split_axis=0,
        concat_axis=0,
        tiled=True,
        axis_index_groups=[list(range(c, spaces, 2)) for c in range(2)],
    ).reshape(spaces // 2 * nodes, members * PAD)
    table_other = lax.ppermute(table, "space", [(i, i ^ 1) for i in range(spaces)])
    rows = -(-PART * (blocks + blocks // members) // 16) * 16
    slopes = pl.pallas_call(
        crps_kernel,
        out_shape=[shape((rows, LANE), BF16)] * members,
        in_specs=[SM] * 2 + [VM] * (4 + members),
        out_specs=[VM] * members,
        scratch_shapes=[
            pltpu.VMEM((spaces * nodes, LANE), F32),
            pltpu.VMEM((members * held + (PAD - PART) * blocks, LANE), F32),
            pltpu.VMEM((members * rows, LANE), F32),
            pltpu.VMEM((2 * LANE, LANE), F32),
            pltpu.VMEM((2 * members * PAD, LANE), F32),
        ],
        compiler_params=params(20),
        cost_estimate=cost(5e9, 6e6, 2e6),
        name="crps",
    )(
        member.astype(jnp.int32).reshape(1),
        ids,
        table,
        table_other,
        seen,
        area.reshape(blocks, LANE),
        *parts,
    )
    slopes = list(slopes)
    for d in (4, 3, 5, 2, 6, 1, 7):
        slopes[d] = lax.ppermute(slopes[d], "ens", [(i, (i - d) % members) for i in range(members)])
    crps, grads = pl.pallas_call(
        unpack_kernel,
        out_shape=(shape((variables, points // members), F32), shape((variables * blocks, LANE), F32)),
        in_specs=[SM] + [VM] * members,
        out_specs=(VM, VM),
        scratch_shapes=[pltpu.VMEM((rows, LANE), F32), pltpu.VMEM((PART * blocks, LANE), F32)],
        compiler_params=params(16),
        cost_estimate=cost(1e6, 2e6),
        name="unpack",
    )(member.astype(jnp.int32).reshape(1), *slopes)
    return crps, grads.reshape(1, variables, points)


def solution(mesh):
    return jax.shard_map(
        local,
        mesh=mesh,
        in_specs=(
            P("ens", None, "space"),
            P("space", None),
            P("space"),
            P("space", None),
            P("space", None),
            P(),
            P(),
            P(),
            P(),
            P(),
            P(),
            P(None, "space"),
            P("space"),
        ),
        out_specs=(P(None, ("space", "ens")), P("ens", None, "space")),
        check_vma=False,
    )
```
